32 devices in a mesh: video: 2 (over y), space: 4 (over z), tm: 4 (over x, core).
Axes of the slice: x: 2, y: 2, z: 4, core: 2. Of those that a mesh axis runs over, the one named last changes fastest.
Arguments:
- spatial_q: bfloat16 [16, 16, 16, 1152], P(('video', 'tm'), 'space'), parts along dimension 0, may hold values from -17 to 17
- spatial_k: bfloat16 [16, 16, 16, 1152], P(('video', 'tm'), 'space'), parts along dimension 0, may hold values from -17 to 17
- spatial_v: bfloat16 [16, 16, 16, 1152], P(('video', 'tm'), 'space'), parts along dimension 0, may hold values from -6 to 6
- temporal_q: bfloat16 [16, 16, 16, 1152], P(('video', 'tm'), 'space'), parts along dimension 0, may hold values from -17 to 17
- temporal_k: bfloat16 [16, 16, 16, 1152], P(('video', 'tm'), 'space'), parts along dimension 0, may hold values from -17 to 17
- temporal_v: bfloat16 [16, 16, 16, 1152], P(('video', 'tm'), 'space'), parts along dimension 0, may hold values from -6 to 6
- key_lists: int32 [16, 8], replicated, may hold values from -1 to 15, as said below
Outputs:
- spatial_out: bfloat16 [16, 16, 16, 1152], P(('video', 'tm'), 'space'), parts along dimension 0
- temporal_out: bfloat16 [16, 16, 16, 1152], P(('video', 'tm'), 'space'), parts along dimension 0
The draws below stay inside these ranges and needn't reach their ends.
There are 2 independent parts, one for each index of `video`. The reference program is written for one: setup_inputs(seed, part) draws one part's arguments, and reference() takes and returns one part's arrays. A program takes and returns all parts, laid end to end along the dimension named above; an argument that names none is the same for every part. Nothing has to cross between parts.
Inputs may be any that keep to these rules, and one draw needn't show every extreme that they name: key_lists[r] names distinct tile rows within 4 rows of r, r itself first; the named entries come first and the rest are -1.
All inputs are finite; a program needn't handle non-finite values.
Results may differ from the reference program's by a relative error of at most 0.0037.
Values may be sent and summed in bfloat16 or wider, within the bound.
No kernel may reach another device: no remote copies, remote signals or barrier semaphores. Data moves between devices by JAX's collectives and lax.ppermute only.
A program may use at most 64 MiB of HBM per device.

```python
import jax
import jax.numpy as jnp
from jax import lax

HEADS = 16
HEAD_DIM = 72
D = 1152
COLS = 16
FRAMES = 8
ROWS = 16
RADIUS = 4
LIST = 8


def drawn_pair(key):
    shape = (FRAMES, ROWS, COLS, D)
    first, second = jax.random.split(key, 2)
    queries = 1.5 * jnp.clip(jax.random.normal(first, shape, jnp.float32), -4.0, 4.0)
    keyset = jnp.clip(jax.random.normal(second, shape, jnp.float32), -4.0, 4.0)
    return (queries, keyset)


def draw_spatial_q(key, part):
    return drawn_pair(jax.random.fold_in(key, 101))[0].astype(jnp.bfloat16)


def draw_spatial_k(key, part):
    return drawn_pair(jax.random.fold_in(key, 101))[1].astype(jnp.bfloat16)


def draw_temporal_q(key, part):
    return drawn_pair(jax.random.fold_in(key, 202))[0].astype(jnp.bfloat16)


def draw_temporal_k(key, part):
    return drawn_pair(jax.random.fold_in(key, 202))[1].astype(jnp.bfloat16)


def draw_key_lists(key, part):
    span = 2 * RADIUS + 1
    offsets = jnp.arange(span, dtype=jnp.int32) - RADIUS
    splits = jax.random.split(key, ROWS + 2)
    orders = jax.vmap(lambda single: jax.random.permutation(single, span))(splits[:ROWS])
    shifted = offsets[orders]
    row_ids = jnp.arange(ROWS, dtype=jnp.int32)[:, None] + shifted
    inside = (row_ids >= 0) & (row_ids < ROWS)
    ranking = jnp.where(shifted == 0, 0, jnp.where(inside, 1, 2)) * 4096 + jnp.arange(span, dtype=jnp.int32)[None, :]
    sorter = jnp.argsort(ranking, axis=1)
    chosen = jnp.take_along_axis(row_ids, sorter, axis=1)[:, :LIST]
    room = jnp.minimum(jnp.sum(inside.astype(jnp.int32), axis=1), LIST)
    counts = jax.random.randint(splits[ROWS], (ROWS,), 1, LIST + 1)
    star = RADIUS + jax.random.randint(splits[ROWS + 1], (), 0, ROWS - 2 * RADIUS)
    counts = jnp.where(jnp.arange(ROWS, dtype=jnp.int32) == star, LIST, counts)
    counts = jnp.minimum(counts, room)
    filled = jnp.arange(LIST, dtype=jnp.int32)[None, :] < counts[:, None]
    return jnp.where(filled, chosen, -1).astype(jnp.int32)


def block_levels(own_key, dims, cuts, low, top_value):
    level = 1.0
    for dim, parts in cuts:
        steps = jax.random.uniform(jax.random.fold_in(jax.random.fold_in(own_key, 6), dim), (parts,), jnp.float32, low / len(cuts), top_value / len(cuts))
        level = level * jnp.repeat(jnp.exp(steps), dims[dim] // parts).reshape((-1,) + (1,) * (len(dims) - 1 - dim))
    return level


def normal_values(stream_key, dims, scale, limit, pieces=(), kind=jnp.bfloat16):
    result = scale * jax.random.normal(stream_key, dims, jnp.float32)
    if pieces:
        result = result * block_levels(stream_key, dims, pieces, -0.22, 0.18)
    return jnp.clip(result, -limit, limit).astype(kind)


def setup_inputs(seed: int = 0, part: int = 0) -> dict:
    keys = jax.random.split(jax.random.key(seed), 8)
    part_keys = jax.random.split(jax.random.fold_in(keys[7], part), 8)
    spatial_q = draw_spatial_q(jax.random.fold_in(jax.random.fold_in(keys[7], part), 71), part)
    spatial_k = draw_spatial_k(jax.random.fold_in(jax.random.fold_in(keys[7], part), 71), part)
    spatial_v = normal_values(part_keys[2], (FRAMES, ROWS, COLS, D), 1.0, 6.0, ((0, 4), (1, 4)))
    temporal_q = draw_temporal_q(jax.random.fold_in(jax.random.fold_in(keys[7], part), 71), part)
    temporal_k = draw_temporal_k(jax.random.fold_in(jax.random.fold_in(keys[7], part), 71), part)
    temporal_v = normal_values(part_keys[5], (FRAMES, ROWS, COLS, D), 1.0, 6.0, ((0, 4), (1, 4)))
    key_lists = draw_key_lists(jax.random.fold_in(keys[7], 71), part)
    return {"spatial_q": spatial_q, "spatial_k": spatial_k, "spatial_v": spatial_v, "temporal_q": temporal_q, "temporal_k": temporal_k, "temporal_v": temporal_v, "key_lists": key_lists}


big_negative = -1.0e30


def spatial_item(item_index, spatial_q, spatial_k, spatial_v, key_lists):
    frame_index = item_index // ROWS
    row_index = item_index % ROWS
    queries = spatial_q[frame_index, row_index].astype(jnp.float32).reshape(COLS, HEADS, HEAD_DIM)
    entries = key_lists[row_index]
    listed = entries >= 0
    safe_rows = jnp.where(listed, entries, 0).astype(jnp.int32)
    keyset = spatial_k[frame_index][safe_rows].astype(jnp.float32).reshape(LIST * COLS, HEADS, HEAD_DIM)
    values = spatial_v[frame_index][safe_rows].astype(jnp.float32).reshape(LIST * COLS, HEADS, HEAD_DIM)
    scores = jnp.einsum("chd,khd->hck", queries, keyset) * HEAD_DIM ** -0.5
    allowed = jnp.repeat(listed, COLS)[None, None, :]
    highest = jnp.max(jnp.where(allowed, scores, big_negative), axis=-1, keepdims=True)
    weights = jnp.where(allowed, jnp.exp(scores - highest), 0.0)
    totals = jnp.sum(weights, axis=-1)
    rounded = lax.optimization_barrier(weights.astype(jnp.bfloat16)).astype(jnp.float32)
    blended = jnp.einsum("hck,khd->chd", rounded, values) / jnp.transpose(totals)[:, :, None]
    return blended.reshape(COLS, D).astype(jnp.bfloat16)


def reference(spatial_q, spatial_k, spatial_v, temporal_q, temporal_k, temporal_v, key_lists):
    def one_item(item_index):
        return spatial_item(item_index, spatial_q, spatial_k, spatial_v, key_lists)

    spatial_out = lax.map(one_item, jnp.arange(FRAMES * ROWS, dtype=jnp.int32))
    spatial_out = spatial_out.reshape(FRAMES, ROWS, COLS, D)

    queries = temporal_q.astype(jnp.float32).reshape(FRAMES, ROWS * COLS, HEADS, HEAD_DIM)
    keyset = temporal_k.astype(jnp.float32).reshape(FRAMES, ROWS * COLS, HEADS, HEAD_DIM)
    values = temporal_v.astype(jnp.float32).reshape(FRAMES, ROWS * COLS, HEADS, HEAD_DIM)
    scores = jnp.einsum("flhd,elhd->lhfe", queries, keyset) * HEAD_DIM ** -0.5
    highest = jnp.max(scores, axis=-1, keepdims=True)
    weights = jnp.exp(scores - highest)
    totals = jnp.sum(weights, axis=-1)
    rounded = lax.optimization_barrier(weights.astype(jnp.bfloat16)).astype(jnp.float32)
    blended = jnp.einsum("lhfe,elhd->flhd", rounded, values) / jnp.transpose(totals, (2, 0, 1))[:, :, :, None]
    temporal_out = blended.reshape(FRAMES, ROWS, COLS, D).astype(jnp.bfloat16)
    return (spatial_out, temporal_out)
```

```python
import functools
import math

import jax
import jax.numpy as jnp
from jax import lax
from jax.experimental import pallas as pl
from jax.experimental.pallas import tpu as pltpu
from jax.sharding import PartitionSpec as P

HEAD_DIM = 72
PAIR = 2 * HEAD_DIM
LANES = 128
WINDOW = 2 * LANES
SCALE = HEAD_DIM ** (-0.5) * math.log2(math.e)
big_negative = -1e30


def shifted(value, axis, by):
    length = lax.axis_size(axis)
    pairs = [(i, i + by) for i in range(length) if 0 <= i + by < length]
    return lax.ppermute(value, axis, pairs)


def gathered(values, axis):
    length = lax.axis_size(axis)
    held = [[value] for value in values]
    step = length // 2
    while step:
        pairs = [(i, i ^ step) for i in range(length)]
        for parts in held:
            parts.extend([lax.ppermute(part, axis, pairs) for part in parts])
        step //= 2
    return held


def head_masks(pair, rows):
    lane = lax.broadcasted_iota(jnp.int32, (rows, WINDOW), 1)
    first = (PAIR - LANES) * pair
    return [
        (lane >= first + head * HEAD_DIM) & (lane < first + (head + 1) * HEAD_DIM)
        for head in range(2)
    ]


def attend_pair(pair, queries, keyset, values, bias):
    rows = queries.shape[0]
    masks = head_masks(pair, rows)
    stacked = jnp.concatenate(
        [jnp.where(mask, queries, jnp.zeros_like(queries)) for mask in masks], axis=0
    )
    scores = lax.dot_general(
        stacked, keyset, (((1,), (1,)), ((), ())), preferred_element_type=jnp.float32
    )
    scores = scores * SCALE + bias
    highest = jnp.max(scores, axis=-1, keepdims=True)
    weights = jnp.exp2(scores - highest)
    totals = jnp.sum(weights, axis=-1, keepdims=True)
    blended = jnp.dot(
        weights.astype(jnp.bfloat16), values, preferred_element_type=jnp.float32
    )
    blended = blended / totals
    zeros = jnp.zeros((rows, WINDOW), jnp.float32)
    return jnp.where(masks[0], blended[:rows], jnp.where(masks[1], blended[rows:], zeros))


def attend(channels, read_queries, read_keys, read_values, bias, write):
    carry = None
    pairs = channels // PAIR
    for pair in range(pairs):
        lanes = slice(pair * LANES, pair * LANES + WINDOW)
        both = attend_pair(
            pair, read_queries(lanes), read_keys(lanes), read_values(lanes), bias
        )
        low = both[:, :LANES]
        if carry is not None:
            low = low + carry
        write(slice(pair * LANES, (pair + 1) * LANES), low.astype(jnp.bfloat16))
        carry = both[:, LANES:]
    write(slice(pairs * LANES, (pairs + 1) * LANES), carry.astype(jnp.bfloat16))


def spatial_kernel(blocks, row_start_ref, lists_ref, q_ref, *refs):
    k_refs, v_refs, out_ref = refs[:blocks], refs[blocks : 2 * blocks], refs[2 * blocks]
    frames, rows, columns, channels = q_ref.shape
    entries = lists_ref.shape[1]
    row_start = row_start_ref[0]
    extent = blocks * rows
    key_rows = lax.broadcasted_iota(jnp.int32, (columns, extent * columns), 1) // columns
    key_rows = key_rows + (row_start - (blocks // 2) * rows)
    bias = []
    for row in range(rows):
        member = key_rows == row_start + row
        for entry in range(entries):
            member = member | (key_rows == lists_ref[row_start + row, entry])
        bias.append(jnp.where(member & (key_rows >= 0), 0.0, big_negative))
    bias = jnp.concatenate(bias + bias, axis=0)
    tokens = rows * columns
    for frame in range(frames):

        def read(chosen, lanes):
            return jnp.concatenate(
                [ref[frame, :, :, lanes].reshape(tokens, WINDOW) for ref in chosen], axis=0
            )

        def write(lanes, value):
            out_ref[frame, :, :, lanes] = value.reshape(rows, columns, LANES)

        attend(
            channels,
            lambda lanes: read([q_ref], lanes),
            lambda lanes: read(k_refs, lanes),
            lambda lanes: read(v_refs, lanes),
            bias,
            write,
        )


def temporal_kernel(blocks, q_ref, *refs):
    k_refs, v_refs, out_ref = refs[:blocks], refs[blocks : 2 * blocks], refs[2 * blocks]
    frames, rows, columns, channels = q_ref.shape
    queries = frames * columns
    shape = (2 * queries, blocks * queries)
    own = lax.broadcasted_iota(jnp.int32, shape, 0) % columns
    other = lax.broadcasted_iota(jnp.int32, shape, 1) % columns
    bias = jnp.where(own == other, 0.0, big_negative)
    for row in range(rows):

        def read(chosen, lanes):
            return jnp.concatenate(
                [ref[:, row, :, lanes].reshape(queries, WINDOW) for ref in chosen], axis=0
            )

        def write(lanes, value):
            out_ref[:, row, :, lanes] = value.reshape(frames, columns, LANES)

        attend(
            channels,
            lambda lanes: read([q_ref], lanes),
            lambda lanes: read(k_refs, lanes),
            lambda lanes: read(v_refs, lanes),
            bias,
            write,
        )


def in_vmem():
    return pl.BlockSpec(memory_space=pltpu.VMEM)


def in_smem():
    return pl.BlockSpec(memory_space=pltpu.SMEM)


def on_device(spatial_q, spatial_k, spatial_v, temporal_q, temporal_k, temporal_v, key_lists):
    frames, rows, columns, channels = spatial_q.shape
    reach = -(-(key_lists.shape[1] // 2) // rows)
    row_start = lax.axis_index("space") * rows
    hops = [by for distance in range(1, reach + 1) for by in (distance, -distance)]
    hops.sort(reverse=True)
    hops.insert(reach, 0)
    temporal_keys, temporal_values = gathered([temporal_k, temporal_v], "tm")
    spatial_keys = [shifted(spatial_k, "space", by) if by else spatial_k for by in hops]
    spatial_values = [shifted(spatial_v, "space", by) if by else spatial_v for by in hops]

    params = pltpu.CompilerParams(vmem_limit_bytes=40 * 1024 * 1024)
    out_shape = jax.ShapeDtypeStruct(spatial_q.shape, jnp.bfloat16)
    blocks = len(hops)
    tokens = frames * rows * columns
    spatial_out = pl.pallas_call(
        functools.partial(spatial_kernel, blocks),
        out_shape=out_shape,
        in_specs=[in_smem(), in_smem()] + [in_vmem()] * (1 + 2 * blocks),
        out_specs=in_vmem(),
        compiler_params=params,
        cost_estimate=pl.CostEstimate(
            flops=4 * tokens * blocks * rows * columns * channels,
            bytes_accessed=(2 + 2 * blocks) * spatial_q.size * 2,
            transcendentals=0,
        ),
        name="spatial",
    )(row_start.reshape(1), key_lists, spatial_q, *spatial_keys, *spatial_values)
    blocks = len(temporal_keys)
    temporal_out = pl.pallas_call(
        functools.partial(temporal_kernel, blocks),
        out_shape=out_shape,
        in_specs=[in_vmem()] * (1 + 2 * blocks),
        out_specs=in_vmem(),
        compiler_params=params,
        cost_estimate=pl.CostEstimate(
            flops=4 * tokens * blocks * frames * columns * channels,
            bytes_accessed=(2 + 2 * blocks) * spatial_q.size * 2,
            transcendentals=0,
        ),
        name="temporal",
    )(temporal_q, *temporal_keys, *temporal_values)
    return (spatial_out, temporal_out)


def solution(mesh):
    placed = P(("video", "tm"), "space", None, None)
    return jax.shard_map(
        on_device,
        mesh=mesh,
        in_specs=(placed,) * 6 + (P(),),
        out_specs=(placed, placed),
        check_vma=False,
    )
```

```python
import functools
import math

import jax
import jax.numpy as jnp
from jax import lax
from jax.experimental import pallas as pl
from jax.experimental.pallas import tpu as pltpu
from jax.sharding import PartitionSpec as P

HEAD_DIM = 72
PAIR = 2 * HEAD_DIM
LANES = 128
WINDOW = 2 * LANES
SCALE = HEAD_DIM ** (-0.5) * math.log2(math.e)
big_negative = -1e30


def partner_of(index, distance, parity):
    upward = (index // distance) % 2 == parity
    if isinstance(index, int):
        return index + distance if upward else index - distance
    return jnp.where(upward, index + distance, index - distance)


def exchanged(value, axis, distance, parity):
    length = lax.axis_size(axis)
    pairs = []
    for index in range(length):
        partner = partner_of(index, distance, parity)
        pairs.append((index, partner if 0 <= partner < length else index))
    return lax.ppermute(value, axis, pairs)


def gathered(value, axis):
    length = lax.axis_size(axis)
    held = [value]
    step = length // 2
    while step:
        pairs = [(i, i ^ step) for i in range(length)]
        held.extend([lax.ppermute(part, axis, pairs) for part in held])
        step //= 2
    return held


def head_masks(pair, rows):
    lane = lax.broadcasted_iota(jnp.int32, (rows, WINDOW), 1)
    first = (PAIR - LANES) * pair
    return [
        (lane >= first + head * HEAD_DIM) & (lane < first + (head + 1) * HEAD_DIM)
        for head in range(2)
    ]


def window_of(pair):
    return slice(pair * LANES, pair * LANES + WINDOW)


def weigh_pair(pair, queries, keyset, bias):
    rows = queries.shape[0]
    masks = head_masks(pair, rows)
    stacked = jnp.concatenate(
        [queries * mask.astype(jnp.bfloat16) for mask in masks], axis=0
    )
    scores = lax.dot_general(
        stacked, keyset, (((1,), (1,)), ((), ())), preferred_element_type=jnp.float32
    )
    scores = scores * SCALE + bias
    highest = jnp.max(scores, axis=-1, keepdims=True)
    weights = jnp.exp2(scores - highest)
    inverse = 1.0 / jnp.sum(weights, axis=-1, keepdims=True)
    inverse = jnp.where(masks[0], inverse[:rows], jnp.where(masks[1], inverse[rows:], 0.0))
    return weights.astype(jnp.bfloat16), inverse


def blend_pairs(pairs, read_weights, read_inverse, read_values, write):
    carry = None
    for pair in range(pairs):
        inverse = read_inverse(pair)
        rows = inverse.shape[0]
        blended = jnp.dot(
            read_weights(pair), read_values(window_of(pair)), preferred_element_type=jnp.float32
        )
        mask = head_masks(pair, rows)[0]
        both = jnp.where(mask, blended[:rows], blended[rows:]) * inverse
        low = both[:, :LANES]
        if carry is not None:
            low = low + carry
        write(slice(pair * LANES, (pair + 1) * LANES), low.astype(jnp.bfloat16))
        carry = both[:, LANES:]
    write(slice(pairs * LANES, (pairs + 1) * LANES), carry.astype(jnp.bfloat16))


def read_tokens(refs, frame, lanes):
    return jnp.concatenate(
        [ref[frame, :, :, lanes].reshape(-1, WINDOW) for ref in refs], axis=0
    )


def read_row(refs, row, lanes):
    return jnp.concatenate([ref[:, row, :, lanes].reshape(-1, WINDOW) for ref in refs], axis=0)


def spatial_weigh_kernel(blocks, space, index_ref, lists_ref, q_ref, *refs):
    k_refs, weights_ref, inverse_ref = refs[:blocks], refs[blocks], refs[blocks + 1]
    frames, rows, columns, channels = q_ref.shape
    index = index_ref[0]
    key_rows = []
    for distance in range(blocks // 2 + 1):
        for parity in range(2 if distance else 1):
            owner = partner_of(index, distance, parity) if distance else index
            first = jnp.where((owner >= 0) & (owner < space), owner * rows, -(2**20))
            row = lax.broadcasted_iota(jnp.int32, (columns, rows * columns), 1) // columns
            key_rows.append(row + first)
    key_rows = jnp.concatenate(key_rows, axis=1)
    bias = []
    for row in range(rows):
        query_row = index * rows + row
        member = key_rows == query_row
        for entry in range(lists_ref.shape[0]):
            member = member | (key_rows == lists_ref[entry, query_row])
        bias.append(jnp.where(member & (key_rows >= 0), 0.0, big_negative))
    bias = jnp.concatenate(bias + bias, axis=0)
    for frame in range(frames):
        for pair in range(channels // PAIR):
            lanes = window_of(pair)
            weights_ref[frame, pair], inverse_ref[frame, pair] = weigh_pair(
                pair, read_tokens([q_ref], frame, lanes), read_tokens(k_refs, frame, lanes), bias
            )


def spatial_blend_kernel(blocks, weights_ref, inverse_ref, *refs):
    v_refs, out_ref = refs[:blocks], refs[blocks]
    frames, rows, columns, channels = out_ref.shape
    for frame in range(frames):

        def write(lanes, value):
            out_ref[frame, :, :, lanes] = value.reshape(rows, columns, LANES)

        blend_pairs(
            channels // PAIR,
            lambda pair: weights_ref[frame, pair],
            lambda pair: inverse_ref[frame, pair],
            lambda lanes: read_tokens(v_refs, frame, lanes),
            write,
        )


def temporal_weigh_kernel(blocks, q_ref, *refs):
    k_refs, weights_ref, inverse_ref = refs[:blocks], refs[blocks], refs[blocks + 1]
    frames, rows, columns, channels = q_ref.shape
    shape = (2 * frames * columns, blocks * frames * columns)
    own = lax.broadcasted_iota(jnp.int32, shape, 0) % columns
    other = lax.broadcasted_iota(jnp.int32, shape, 1) % columns
    bias = jnp.where(own == other, 0.0, big_negative)
    for row in range(rows):
        for pair in range(channels // PAIR):
            lanes = window_of(pair)
            weights_ref[row, pair], inverse_ref[row, pair] = weigh_pair(
                pair, read_row([q_ref], row, lanes), read_row(k_refs, row, lanes), bias
            )


def temporal_blend_kernel(blocks, weights_ref, inverse_ref, *refs):
    v_refs, out_ref = refs[:blocks], refs[blocks]
    frames, rows, columns, channels = out_ref.shape
    for row in range(rows):

        def write(lanes, value):
            out_ref[:, row, :, lanes] = value.reshape(frames, columns, LANES)

        blend_pairs(
            channels // PAIR,
            lambda pair: weights_ref[row, pair],
            lambda pair: inverse_ref[row, pair],
            lambda lanes: read_row(v_refs, row, lanes),
            write,
        )


def call(kernel, name, out_shape, scalars, arrays, flops):
    in_vmem = pl.BlockSpec(memory_space=pltpu.VMEM)
    in_smem = pl.BlockSpec(memory_space=pltpu.SMEM)
    return pl.pallas_call(
        kernel,
        out_shape=out_shape,
        in_specs=[in_smem] * len(scalars) + [in_vmem] * len(arrays),
        out_specs=jax.tree.map(lambda _: in_vmem, out_shape),
        compiler_params=pltpu.CompilerParams(vmem_limit_bytes=40 * 1024 * 1024),
        cost_estimate=pl.CostEstimate(
            flops=flops, bytes_accessed=sum(2 * a.size for a in arrays), transcendentals=0
        ),
        name=name,
    )(*scalars, *arrays)


def weigh_shapes(groups, channels, queries, keys):
    pairs = channels // PAIR
    return (
        jax.ShapeDtypeStruct((groups, pairs, 2 * queries, keys), jnp.bfloat16),
        jax.ShapeDtypeStruct((groups, pairs, queries, WINDOW), jnp.float32),
    )


def on_device(spatial_q, spatial_k, spatial_v, temporal_q, temporal_k, temporal_v, key_lists):
    frames, rows, columns, channels = spatial_q.shape
    space = lax.axis_size("space")
    reach = -(-(key_lists.shape[1] // 2) // rows)
    index = lax.axis_index("space").reshape(1)
    out_shape = jax.ShapeDtypeStruct(spatial_q.shape, jnp.bfloat16)
    tokens = frames * rows * columns

    def halo(value):
        return [value] + [
            exchanged(value, "space", distance, parity)
            for distance in range(1, reach + 1)
            for parity in range(2)
        ]

    temporal_keys = gathered(temporal_k, "tm")
    spatial_keys = halo(spatial_k)
    temporal_values = gathered(temporal_v, "tm")
    spatial_values = halo(spatial_v)

    blocks = len(spatial_keys)
    keys = blocks * rows * columns
    flops = 2 * tokens * keys * channels
    weights, inverse = call(
        functools.partial(spatial_weigh_kernel, blocks, space),
        "spatial_weigh",
        weigh_shapes(frames, channels, rows * columns, keys),
        [index, key_lists.T],
        [spatial_q, *spatial_keys],
        flops,
    )
    spatial_out = call(
        functools.partial(spatial_blend_kernel, blocks),
        "spatial_blend",
        out_shape,
        [],
        [weights, inverse, *spatial_values],
        flops,
    )
    blocks = len(temporal_keys)
    keys = blocks * frames * columns
    flops = 2 * tokens * keys * channels
    weights, inverse = call(
        functools.partial(temporal_weigh_kernel, blocks),
        "temporal_weigh",
        weigh_shapes(rows, channels, frames * columns, keys),
        [],
        [temporal_q, *temporal_keys],
        flops,
    )
    temporal_out = call(
        functools.partial(temporal_blend_kernel, blocks),
        "temporal_blend",
        out_shape,
        [],
        [weights, inverse, *temporal_values],
        flops,
    )
    return (spatial_out, temporal_out)


def solution(mesh):
    placed = P(("video", "tm"), "space", None, None)
    return jax.shard_map(
        on_device,
        mesh=mesh,
        in_specs=(placed,) * 6 + (P(),),
        out_specs=(placed, placed),
        check_vma=False,
    )
```

```python
import functools
import math

import jax
import jax.numpy as jnp
from jax import lax
from jax.experimental import pallas as pl
from jax.experimental.pallas import tpu as pltpu
from jax.sharding import PartitionSpec as P

HEAD_DIM = 72
PAIR = 2 * HEAD_DIM
LANES = 128
WINDOW = 2 * LANES
SCALE = HEAD_DIM ** (-0.5) * math.log2(math.e)
big_negative = -1e30


def partner_of(index, distance, parity):
    upward = (index // distance) % 2 == parity
    if isinstance(index, int):
        return index + distance if upward else index - distance
    return jnp.where(upward, index + distance, index - distance)


def exchanged(value, axis, distance, parity):
    length = lax.axis_size(axis)
    pairs = []
    for index in range(length):
        partner = partner_of(index, distance, parity)
        pairs.append((index, partner if 0 <= partner < length else index))
    return lax.ppermute(value, axis, pairs)


def gathered(value, axis):
    return [lax.all_gather(value, axis, axis=0, tiled=True)]


def head_masks(pair, rows):
    lane = lax.broadcasted_iota(jnp.int32, (rows, WINDOW), 1)
    first = (PAIR - LANES) * pair
    return [
        (lane >= first + head * HEAD_DIM) & (lane < first + (head + 1) * HEAD_DIM)
        for head in range(2)
    ]


def window_of(pair):
    return slice(pair * LANES, pair * LANES + WINDOW)


def weigh_pair(pair, queries, keyset, bias):
    rows = queries.shape[0]
    masks = head_masks(pair, rows)
    stacked = jnp.concatenate(
        [queries * mask.astype(jnp.bfloat16) for mask in masks], axis=0
    )
    scores = lax.dot_general(
        stacked, keyset, (((1,), (1,)), ((), ())), preferred_element_type=jnp.float32
    )
    scores = scores * SCALE + bias
    highest = jnp.max(scores, axis=-1, keepdims=True)
    weights = jnp.exp2(scores - highest)
    inverse = 1.0 / jnp.sum(weights, axis=-1, keepdims=True)
    inverse = jnp.where(masks[0], inverse[:rows], jnp.where(masks[1], inverse[rows:], 0.0))
    return weights.astype(jnp.bfloat16), inverse


def blend_pairs(pairs, read_weights, read_inverse, read_values, write):
    carry = None
    for pair in range(pairs):
        inverse = read_inverse(pair)
        rows = inverse.shape[0]
        blended = jnp.dot(
            read_weights(pair), read_values(window_of(pair)), preferred_element_type=jnp.float32
        )
        mask = head_masks(pair, rows)[0]
        both = jnp.where(mask, blended[:rows], blended[rows:]) * inverse
        low = both[:, :LANES]
        if carry is not None:
            low = low + carry
        write(slice(pair * LANES, (pair + 1) * LANES), low.astype(jnp.bfloat16))
        carry = both[:, LANES:]
    write(slice(pairs * LANES, (pairs + 1) * LANES), carry.astype(jnp.bfloat16))


def read_tokens(refs, frame, lanes):
    return jnp.concatenate(
        [ref[frame, :, :, lanes].reshape(-1, WINDOW) for ref in refs], axis=0
    )


def read_row(refs, row, lanes):
    return jnp.concatenate([ref[:, row, :, lanes].reshape(-1, WINDOW) for ref in refs], axis=0)


def spatial_weigh_kernel(blocks, space, index_ref, lists_ref, q_ref, *refs):
    k_refs, weights_ref, inverse_ref = refs[:blocks], refs[blocks], refs[blocks + 1]
    frames, rows, columns, channels = q_ref.shape
    index = index_ref[0]
    key_rows = []
    for distance in range(blocks // 2 + 1):
        for parity in range(2 if distance else 1):
            owner = partner_of(index, distance, parity) if distance else index
            first = jnp.where((owner >= 0) & (owner < space), owner * rows, -(2**20))
            row = lax.broadcasted_iota(jnp.int32, (columns, rows * columns), 1) // columns
            key_rows.append(row + first)
    key_rows = jnp.concatenate(key_rows, axis=1)
    bias = []
    for row in range(rows):
        query_row = index * rows + row
        member = key_rows == query_row
        for entry in range(lists_ref.shape[0]):
            member = member | (key_rows == lists_ref[entry, query_row])
        bias.append(jnp.where(member & (key_rows >= 0), 0.0, big_negative))
    bias = jnp.concatenate(bias + bias, axis=0)
    for frame in range(frames):
        for pair in range(channels // PAIR):
            lanes = window_of(pair)
            weights_ref[frame, pair], inverse_ref[frame, pair] = weigh_pair(
                pair, read_tokens([q_ref], frame, lanes), read_tokens(k_refs, frame, lanes), bias
            )


def spatial_blend_kernel(blocks, weights_ref, inverse_ref, *refs):
    v_refs, out_ref = refs[:blocks], refs[blocks]
    frames, rows, columns, channels = out_ref.shape
    for frame in range(frames):

        def write(lanes, value):
            out_ref[frame, :, :, lanes] = value.reshape(rows, columns, LANES)

        blend_pairs(
            channels // PAIR,
            lambda pair: weights_ref[frame, pair],
            lambda pair: inverse_ref[frame, pair],
            lambda lanes: read_tokens(v_refs, frame, lanes),
            write,
        )


def temporal_weigh_kernel(blocks, q_ref, *refs):
    k_refs, weights_ref, inverse_ref = refs[:blocks], refs[blocks], refs[blocks + 1]
    frames, rows, columns, channels = q_ref.shape
    shape = (2 * frames * columns, blocks * k_refs[0].shape[0] * columns)
    own = lax.broadcasted_iota(jnp.int32, shape, 0) % columns
    other = lax.broadcasted_iota(jnp.int32, shape, 1) % columns
    bias = jnp.where(own == other, 0.0, big_negative)
    for row in range(rows):
        for pair in range(channels // PAIR):
            lanes = window_of(pair)
            weights_ref[row, pair], inverse_ref[row, pair] = weigh_pair(
                pair, read_row([q_ref], row, lanes), read_row(k_refs, row, lanes), bias
            )


def temporal_blend_kernel(blocks, weights_ref, inverse_ref, *refs):
    v_refs, out_ref = refs[:blocks], refs[blocks]
    frames, rows, columns, channels = out_ref.shape
    for row in range(rows):

        def write(lanes, value):
            out_ref[:, row, :, lanes] = value.reshape(frames, columns, LANES)

        blend_pairs(
            channels // PAIR,
            lambda pair: weights_ref[row, pair],
            lambda pair: inverse_ref[row, pair],
            lambda lanes: read_row(v_refs, row, lanes),
            write,
        )


def call(kernel, name, out_shape, scalars, arrays, flops):
    in_vmem = pl.BlockSpec(memory_space=pltpu.VMEM)
    in_smem = pl.BlockSpec(memory_space=pltpu.SMEM)
    return pl.pallas_call(
        kernel,
        out_shape=out_shape,
        in_specs=[in_smem] * len(scalars) + [in_vmem] * len(arrays),
        out_specs=jax.tree.map(lambda _: in_vmem, out_shape),
        compiler_params=pltpu.CompilerParams(vmem_limit_bytes=40 * 1024 * 1024),
        cost_estimate=pl.CostEstimate(
            flops=flops, bytes_accessed=sum(2 * a.size for a in arrays), transcendentals=0
        ),
        name=name,
    )(*scalars, *arrays)


def weigh_shapes(groups, channels, queries, keys):
    pairs = channels // PAIR
    return (
        jax.ShapeDtypeStruct((groups, pairs, 2 * queries, keys), jnp.bfloat16),
        jax.ShapeDtypeStruct((groups, pairs, queries, WINDOW), jnp.float32),
    )


def on_device(spatial_q, spatial_k, spatial_v, temporal_q, temporal_k, temporal_v, key_lists):
    frames, rows, columns, channels = spatial_q.shape
    space = lax.axis_size("space")
    reach = -(-(key_lists.shape[1] // 2) // rows)
    index = lax.axis_index("space").reshape(1)
    out_shape = jax.ShapeDtypeStruct(spatial_q.shape, jnp.bfloat16)
    tokens = frames * rows * columns

    def halo(value):
        return [value] + [
            exchanged(value, "space", distance, parity)
            for distance in range(1, reach + 1)
            for parity in range(2)
        ]

    temporal_keys = gathered(temporal_k, "tm")
    spatial_keys = halo(spatial_k)
    temporal_values = gathered(temporal_v, "tm")
    spatial_values = halo(spatial_v)

    blocks = len(spatial_keys)
    keys = blocks * rows * columns
    flops = 2 * tokens * keys * channels
    weights, inverse = call(
        functools.partial(spatial_weigh_kernel, blocks, space),
        "spatial_weigh",
        weigh_shapes(frames, channels, rows * columns, keys),
        [index, key_lists.T],
        [spatial_q, *spatial_keys],
        flops,
    )
    spatial_out = call(
        functools.partial(spatial_blend_kernel, blocks),
        "spatial_blend",
        out_shape,
        [],
        [weights, inverse, *spatial_values],
        flops,
    )
    blocks = len(temporal_keys)
    keys = temporal_keys[0].shape[0] * columns
    flops = 2 * tokens * keys * channels
    weights, inverse = call(
        functools.partial(temporal_weigh_kernel, blocks),
        "temporal_weigh",
        weigh_shapes(rows, channels, frames * columns, keys),
        [],
        [temporal_q, *temporal_keys],
        flops,
    )
    temporal_out = call(
        functools.partial(temporal_blend_kernel, blocks),
        "temporal_blend",
        out_shape,
        [],
        [weights, inverse, *temporal_values],
        flops,
    )
    return (spatial_out, temporal_out)


def solution(mesh):
    placed = P(("video", "tm"), "space", None, None)
    return jax.shard_map(
        on_device,
        mesh=mesh,
        in_specs=(placed,) * 6 + (P(),),
        out_specs=(placed, placed),
        check_vma=False,
    )
```

```python
import functools
import math

import jax
import jax.numpy as jnp
from jax import lax
from jax.experimental import pallas as pl
from jax.experimental.pallas import tpu as pltpu
from jax.sharding import PartitionSpec as P

HEAD_DIM = 72
PAIR = 2 * HEAD_DIM
LANES = 128
WINDOW = 2 * LANES
SCALE = HEAD_DIM ** (-0.5) * math.log2(math.e)
big_negative = -1e30


def partner_of(index, distance, parity):
    upward = (index // distance) % 2 == parity
    if isinstance(index, int):
        return index + distance if upward else index - distance
    return jnp.where(upward, index + distance, index - distance)


def exchanged(value, axis, distance, parity):
    length = lax.axis_size(axis)
    pairs = []
    for index in range(length):
        partner = partner_of(index, distance, parity)
        pairs.append((index, partner if 0 <= partner < length else index))
    return lax.ppermute(value, axis, pairs)


def swapped(value, axis, step):
    return lax.ppermute(value, axis, [(i, i ^ step) for i in range(lax.axis_size(axis))])


def head_masks(pair, rows):
    lane = lax.broadcasted_iota(jnp.int32, (rows, WINDOW), 1)
    first = (PAIR - LANES) * pair
    return [
        (lane >= first + head * HEAD_DIM) & (lane < first + (head + 1) * HEAD_DIM)
        for head in range(2)
    ]


def window_of(pair):
    return slice(pair * LANES, pair * LANES + WINDOW)


def weigh_pair(pair, queries, keyset, bias):
    rows = queries.shape[0]
    masks = head_masks(pair, rows)
    stacked = jnp.concatenate(
        [queries * mask.astype(jnp.bfloat16) for mask in masks], axis=0
    )
    scores = lax.dot_general(
        stacked, keyset, (((1,), (1,)), ((), ())), preferred_element_type=jnp.float32
    )
    scores = scores * SCALE + bias
    highest = jnp.max(scores, axis=-1, keepdims=True)
    weights = jnp.exp2(scores - highest)
    inverse = 1.0 / jnp.sum(weights, axis=-1, keepdims=True)
    inverse = jnp.where(masks[0], inverse[:rows], jnp.where(masks[1], inverse[rows:], 0.0))
    return weights.astype(jnp.bfloat16), inverse


def blend_pairs(pairs, read_weights, read_inverse, read_values, write):
    carry = None
    for pair in range(pairs):
        inverse = read_inverse(pair)
        rows = inverse.shape[0]
        blended = jnp.dot(
            read_weights(pair), read_values(window_of(pair)), preferred_element_type=jnp.float32
        )
        mask = head_masks(pair, rows)[0]
        both = jnp.where(mask, blended[:rows], blended[rows:]) * inverse
        low = both[:, :LANES]
        if carry is not None:
            low = low + carry
        write(slice(pair * LANES, (pair + 1) * LANES), low.astype(jnp.bfloat16))
        carry = both[:, LANES:]
    write(slice(pairs * LANES, (pairs + 1) * LANES), carry.astype(jnp.bfloat16))


def read_tokens(refs, frame, lanes):
    return jnp.concatenate(
        [ref[frame, :, :, lanes].reshape(-1, WINDOW) for ref in refs], axis=0
    )


def read_row(refs, row, lanes):
    return jnp.concatenate([ref[:, row, :, lanes].reshape(-1, WINDOW) for ref in refs], axis=0)


def spatial_weigh_kernel(blocks, space, index_ref, lists_ref, q_ref, *refs):
    k_refs, weights_ref, inverse_ref = refs[:blocks], *refs[-2:]
    frames, rows, columns, channels = q_ref.shape
    index = index_ref[0]
    key_rows = []
    for distance in range(blocks // 2 + 1):
        for parity in range(2 if distance else 1):
            owner = partner_of(index, distance, parity) if distance else index
            first = jnp.where((owner >= 0) & (owner < space), owner * rows, -(2**20))
            row = lax.broadcasted_iota(jnp.int32, (columns, rows * columns), 1) // columns
            key_rows.append(row + first)
    key_rows = jnp.concatenate(key_rows, axis=1)
    bias = []
    for row in range(rows):
        query_row = index * rows + row
        member = key_rows == query_row
        for entry in range(lists_ref.shape[0]):
            member = member | (key_rows == lists_ref[entry, query_row])
        bias.append(jnp.where(member & (key_rows >= 0), 0.0, big_negative))
    bias = jnp.concatenate(bias + bias, axis=0)
    for frame in range(frames):
        for pair in range(channels // PAIR):
            lanes = window_of(pair)
            weights_ref[frame, pair], inverse_ref[frame, pair] = weigh_pair(
                pair, read_tokens([q_ref], frame, lanes), read_tokens(k_refs, frame, lanes), bias
            )


def spatial_blend_kernel(blocks, weights_ref, inverse_ref, *refs):
    v_refs, out_ref = refs[:blocks], refs[blocks]
    frames, rows, columns, channels = out_ref.shape
    for frame in range(frames):

        def write(lanes, value):
            out_ref[frame, :, :, lanes] = value.reshape(rows, columns, LANES)

        blend_pairs(
            channels // PAIR,
            lambda pair: weights_ref[frame, pair],
            lambda pair: inverse_ref[frame, pair],
            lambda lanes: read_tokens(v_refs, frame, lanes),
            write,
        )


def temporal_weigh_kernel(blocks, q_ref, *refs):
    k_refs, weights_ref, inverse_ref = refs[:blocks], *refs[-2:]
    frames, rows, columns, channels = q_ref.shape
    shape = (2 * frames * columns, sum(ref.shape[0] for ref in k_refs) * columns)
    own = lax.broadcasted_iota(jnp.int32, shape, 0) % columns
    other = lax.broadcasted_iota(jnp.int32, shape, 1) % columns
    bias = jnp.where(own == other, 0.0, big_negative)
    for row in range(rows):
        for pair in range(channels // PAIR):
            lanes = window_of(pair)
            weights_ref[row, pair], inverse_ref[row, pair] = weigh_pair(
                pair, read_row([q_ref], row, lanes), read_row(k_refs, row, lanes), bias
            )


def temporal_blend_kernel(blocks, weights_ref, inverse_ref, *refs):
    v_refs, out_ref = refs[:blocks], refs[blocks]
    frames, rows, columns, channels = out_ref.shape
    for row in range(rows):

        def write(lanes, value):
            out_ref[:, row, :, lanes] = value.reshape(frames, columns, LANES)

        blend_pairs(
            channels // PAIR,
            lambda pair: weights_ref[row, pair],
            lambda pair: inverse_ref[row, pair],
            lambda lanes: read_row(v_refs, row, lanes),
            write,
        )


def call(kernel, name, out_shape, scalars, arrays, flops, others=()):
    in_vmem = pl.BlockSpec(memory_space=pltpu.VMEM)
    in_smem = pl.BlockSpec(memory_space=pltpu.SMEM)
    anywhere = pl.BlockSpec(memory_space=pl.ANY)
    return pl.pallas_call(
        kernel,
        out_shape=out_shape,
        in_specs=[in_smem] * len(scalars) + [in_vmem] * len(arrays) + [anywhere] * len(others),
        out_specs=jax.tree.map(lambda _: in_vmem, out_shape),
        compiler_params=pltpu.CompilerParams(vmem_limit_bytes=40 * 1024 * 1024),
        cost_estimate=pl.CostEstimate(
            flops=flops, bytes_accessed=1, transcendentals=0
        ),
        name=name,
    )(*scalars, *arrays, *others)


def join_kernel(count, *refs):
    out_ref = refs[-1]
    first = 0
    for ref in refs[:count]:
        out_ref[first : first + ref.shape[0]] = ref[...]
        first += ref.shape[0]


def joined(arrays, others):
    shape = (sum(a.shape[0] for a in arrays),) + arrays[0].shape[1:]
    return call(
        functools.partial(join_kernel, len(arrays)),
        "join",
        jax.ShapeDtypeStruct(shape, arrays[0].dtype),
        [],
        arrays,
        1,
        others,
    )


def weigh_shapes(groups, channels, queries, keys):
    pairs = channels // PAIR
    return (
        jax.ShapeDtypeStruct((groups, pairs, 2 * queries, keys), jnp.bfloat16),
        jax.ShapeDtypeStruct((groups, pairs, queries, WINDOW), jnp.float32),
    )


def on_device(spatial_q, spatial_k, spatial_v, temporal_q, temporal_k, temporal_v, key_lists):
    frames, rows, columns, channels = spatial_q.shape
    space = lax.axis_size("space")
    reach = -(-(key_lists.shape[1] // 2) // rows)
    index = lax.axis_index("space").reshape(1)
    out_shape = jax.ShapeDtypeStruct(spatial_q.shape, jnp.bfloat16)
    tokens = frames * rows * columns
    first_step = lax.axis_size("tm") // 2

    def halo(value):
        return [value] + [
            exchanged(value, "space", distance, parity)
            for distance in range(1, reach + 1)
            for parity in range(2)
        ]

    def gathered(own, received, others):
        held, step = [own, received], first_step // 2
        while step:
            held = [joined(held, others)]
            held.append(swapped(held[0], "tm", step))
            step //= 2
        return held

    received_keys = swapped(temporal_k, "tm", first_step)
    received_values = swapped(temporal_v, "tm", first_step)
    spatial_keys = halo(spatial_k)
    spatial_values = halo(spatial_v)

    blocks = len(spatial_keys)
    keys = blocks * rows * columns
    flops = 2 * tokens * keys * channels
    spatial_weights, spatial_inverse = call(
        functools.partial(spatial_weigh_kernel, blocks, space),
        "spatial_weigh",
        weigh_shapes(frames, channels, rows * columns, keys),
        [index, key_lists.T],
        [spatial_q, *spatial_keys],
        1,
        [],
    )
    temporal_keys = gathered(temporal_k, received_keys, [spatial_weights])
    blocks = len(temporal_keys)
    keys = sum(k.shape[0] for k in temporal_keys) * columns
    temporal_weights, temporal_inverse = call(
        functools.partial(temporal_weigh_kernel, blocks),
        "temporal_weigh",
        weigh_shapes(rows, channels, frames * columns, keys),
        [],
        [temporal_q, *temporal_keys],
        1,
    )
    temporal_values = gathered(temporal_v, received_values, [spatial_weights, *spatial_values[1:]])
    spatial_out = call(
        functools.partial(spatial_blend_kernel, len(spatial_values)),
        "spatial_blend",
        out_shape,
        [],
        [spatial_weights, spatial_inverse, *spatial_values],
        1,
    )
    temporal_out = call(
        functools.partial(temporal_blend_kernel, blocks),
        "temporal_blend",
        out_shape,
        [],
        [temporal_weights, temporal_inverse, *temporal_values],
        1,
    )
    return (spatial_out, temporal_out)


def solution(mesh):
    placed = P(("video", "tm"), "space", None, None)
    return jax.shard_map(
        on_device,
        mesh=mesh,
        in_specs=(placed,) * 6 + (P(),),
        out_specs=(placed, placed),
        check_vma=False,
    )
```

```python
import functools
import math

import jax
import jax.numpy as jnp
from jax import lax
from jax.experimental import pallas as pl
from jax.experimental.pallas import tpu as pltpu
from jax.sharding import PartitionSpec as P

HEAD_DIM = 72
PAIR = 2 * HEAD_DIM
LANES = 128
WINDOW = 2 * LANES
SCALE = HEAD_DIM ** (-0.5) * math.log2(math.e)
big_negative = -1e30


def partner_of(index, distance, parity):
    upward = (index // distance) % 2 == parity
    if isinstance(index, int):
        return index + distance if upward else index - distance
    return jnp.where(upward, index + distance, index - distance)


def exchanged(value, axis, distance, parity):
    length = lax.axis_size(axis)
    pairs = []
    for index in range(length):
        partner = partner_of(index, distance, parity)
        pairs.append((index, partner if 0 <= partner < length else index))
    return lax.ppermute(value, axis, pairs)


def swapped(value, axis, step):
    return lax.ppermute(value, axis, [(i, i ^ step) for i in range(lax.axis_size(axis))])


def head_masks(pair, rows):
    lane = lax.broadcasted_iota(jnp.int32, (rows, WINDOW), 1)
    first = (PAIR - LANES) * pair
    return [
        (lane >= first + head * HEAD_DIM) & (lane < first + (head + 1) * HEAD_DIM)
        for head in range(2)
    ]


def window_of(pair):
    return slice(pair * LANES, pair * LANES + WINDOW)


def weigh_pair(pair, queries, keyset, bias):
    rows = queries.shape[0]
    masks = head_masks(pair, rows)
    stacked = jnp.concatenate(
        [queries * mask.astype(jnp.bfloat16) for mask in masks], axis=0
    )
    scores = lax.dot_general(
        stacked, keyset, (((1,), (1,)), ((), ())), preferred_element_type=jnp.float32
    )
    scores = scores * SCALE + bias
    highest = jnp.max(scores, axis=-1, keepdims=True)
    weights = jnp.exp2(scores - highest)
    inverse = 1.0 / jnp.sum(weights, axis=-1, keepdims=True)
    inverse = jnp.where(masks[0], inverse[:rows], jnp.where(masks[1], inverse[rows:], 0.0))
    return weights.astype(jnp.bfloat16), inverse


def blend_pairs(pairs, read_weights, read_inverse, read_values, write):
    carry = None
    for pair in range(pairs):
        inverse = read_inverse(pair)
        rows = inverse.shape[0]
        blended = jnp.dot(
            read_weights(pair), read_values(window_of(pair)), preferred_element_type=jnp.float32
        )
        mask = head_masks(pair, rows)[0]
        both = jnp.where(mask, blended[:rows], blended[rows:]) * inverse
        low = both[:, :LANES]
        if carry is not None:
            low = low + carry
        write(slice(pair * LANES, (pair + 1) * LANES), low.astype(jnp.bfloat16))
        carry = both[:, LANES:]
    write(slice(pairs * LANES, (pairs + 1) * LANES), carry.astype(jnp.bfloat16))


def read_tokens(refs, frame, lanes):
    return jnp.concatenate(
        [ref[frame, :, :, lanes].reshape(-1, WINDOW) for ref in refs], axis=0
    )


def read_row(refs, row, lanes):
    return jnp.concatenate([ref[:, row, :, lanes].reshape(-1, WINDOW) for ref in refs], axis=0)


def spatial_weigh_kernel(blocks, space, index_ref, lists_ref, q_ref, *refs):
    k_refs, weights_ref, inverse_ref = refs[:blocks], *refs[-2:]
    frames, rows, columns, channels = q_ref.shape
    index = index_ref[0]
    key_rows = []
    for distance in range(blocks // 2 + 1):
        for parity in range(2 if distance else 1):
            owner = partner_of(index, distance, parity) if distance else index
            first = jnp.where((owner >= 0) & (owner < space), owner * rows, -(2**20))
            row = lax.broadcasted_iota(jnp.int32, (columns, rows * columns), 1) // columns
            key_rows.append(row + first)
    key_rows = jnp.concatenate(key_rows, axis=1)
    bias = []
    for row in range(rows):
        query_row = index * rows + row
        member = key_rows == query_row
        for entry in range(lists_ref.shape[0]):
            member = member | (key_rows == lists_ref[entry, query_row])
        bias.append(jnp.where(member & (key_rows >= 0), 0.0, big_negative))
    bias = jnp.concatenate(bias + bias, axis=0)
    for frame in range(frames):
        for pair in range(channels // PAIR):
            lanes = window_of(pair)
            weights_ref[frame, pair], inverse_ref[frame, pair] = weigh_pair(
                pair, read_tokens([q_ref], frame, lanes), read_tokens(k_refs, frame, lanes), bias
            )


def spatial_blend_kernel(blocks, weights_ref, inverse_ref, *refs):
    v_refs, out_ref = refs[:blocks], refs[blocks]
    frames, rows, columns, channels = out_ref.shape
    for frame in range(frames):

        def write(lanes, value):
            out_ref[frame, :, :, lanes] = value.reshape(rows, columns, LANES)

        blend_pairs(
            channels // PAIR,
            lambda pair: weights_ref[frame, pair],
            lambda pair: inverse_ref[frame, pair],
            lambda lanes: read_tokens(v_refs, frame, lanes),
            write,
        )


def temporal_weigh_kernel(blocks, q_ref, *refs):
    k_refs, weights_ref, inverse_ref = refs[:blocks], *refs[-2:]
    frames, rows, columns, channels = q_ref.shape
    shape = (2 * frames * columns, sum(ref.shape[0] for ref in k_refs) * columns)
    own = lax.broadcasted_iota(jnp.int32, shape, 0) % columns
    other = lax.broadcasted_iota(jnp.int32, shape, 1) % columns
    bias = jnp.where(own == other, 0.0, big_negative)
    for row in range(rows):
        for pair in range(channels // PAIR):
            lanes = window_of(pair)
            weights_ref[row, pair], inverse_ref[row, pair] = weigh_pair(
                pair, read_row([q_ref], row, lanes), read_row(k_refs, row, lanes), bias
            )


def temporal_blend_kernel(blocks, weights_ref, inverse_ref, *refs):
    v_refs, out_ref = refs[:blocks], refs[blocks]
    frames, rows, columns, channels = out_ref.shape
    for row in range(rows):

        def write(lanes, value):
            out_ref[:, row, :, lanes] = value.reshape(frames, columns, LANES)

        blend_pairs(
            channels // PAIR,
            lambda pair: weights_ref[row, pair],
            lambda pair: inverse_ref[row, pair],
            lambda lanes: read_row(v_refs, row, lanes),
            write,
        )


def call(kernel, name, out_shape, scalars, arrays, flops, others=()):
    in_vmem = pl.BlockSpec(memory_space=pltpu.VMEM)
    in_smem = pl.BlockSpec(memory_space=pltpu.SMEM)
    anywhere = pl.BlockSpec(memory_space=pl.ANY)
    return pl.pallas_call(
        kernel,
        out_shape=out_shape,
        in_specs=[in_smem] * len(scalars) + [in_vmem] * len(arrays) + [anywhere] * len(others),
        out_specs=jax.tree.map(lambda _: in_vmem, out_shape),
        compiler_params=pltpu.CompilerParams(vmem_limit_bytes=40 * 1024 * 1024),
        cost_estimate=pl.CostEstimate(
            flops=flops, bytes_accessed=1, transcendentals=0
        ),
        name=name,
    )(*scalars, *arrays, *others)


def join_kernel(count, *refs):
    out_ref = refs[-1]
    first = 0
    for ref in refs[:count]:
        out_ref[first : first + ref.shape[0]] = ref[...]
        first += ref.shape[0]


def joined(arrays, others):
    shape = (sum(a.shape[0] for a in arrays),) + arrays[0].shape[1:]
    return call(
        functools.partial(join_kernel, len(arrays)),
        "join",
        jax.ShapeDtypeStruct(shape, arrays[0].dtype),
        [],
        arrays,
        1,
        others,
    )


def weigh_shapes(groups, channels, queries, keys):
    pairs = channels // PAIR
    return (
        jax.ShapeDtypeStruct((groups, pairs, 2 * queries, keys), jnp.bfloat16),
        jax.ShapeDtypeStruct((groups, pairs, queries, WINDOW), jnp.float32),
    )


def on_device(spatial_q, spatial_k, spatial_v, temporal_q, temporal_k, temporal_v, key_lists):
    frames, rows, columns, channels = spatial_q.shape
    space = lax.axis_size("space")
    reach = -(-(key_lists.shape[1] // 2) // rows)
    index = lax.axis_index("space").reshape(1)
    out_shape = jax.ShapeDtypeStruct(spatial_q.shape, jnp.bfloat16)
    tokens = frames * rows * columns
    first_step = lax.axis_size("tm") // 2

    def halo(value):
        return [value] + [
            exchanged(value, "space", distance, parity)
            for distance in range(1, reach + 1)
            for parity in range(2)
        ]

    def gathered(own, received, others):
        held, step = [own, received], first_step // 2
        while step:
            held = [joined(held, others)]
            held.append(swapped(held[0], "tm", step))
            step //= 2
        return held

    received_keys = swapped(temporal_k, "tm", first_step)
    received_values = swapped(temporal_v, "tm", first_step)
    spatial_keys = halo(spatial_k)
    spatial_values = halo(spatial_v)

    blocks = len(spatial_keys)
    keys = blocks * rows * columns
    flops = 2 * tokens * keys * channels
    spatial_weights, spatial_inverse = call(
        functools.partial(spatial_weigh_kernel, blocks, space),
        "spatial_weigh",
        weigh_shapes(frames, channels, rows * columns, keys),
        [index, key_lists.T],
        [spatial_q, *spatial_keys],
        1,
        [received_keys],
    )
    temporal_keys = gathered(temporal_k, received_keys, [spatial_weights])
    blocks = len(temporal_keys)
    keys = sum(k.shape[0] for k in temporal_keys) * columns
    temporal_weights, temporal_inverse = call(
        functools.partial(temporal_weigh_kernel, blocks),
        "temporal_weigh",
        weigh_shapes(rows, channels, frames * columns, keys),
        [],
        [temporal_q, *temporal_keys],
        1,
    )
    temporal_values = gathered(temporal_v, received_values, [spatial_weights, *spatial_values[1:]])
    spatial_out = call(
        functools.partial(spatial_blend_kernel, len(spatial_values)),
        "spatial_blend",
        out_shape,
        [],
        [spatial_weights, spatial_inverse, *spatial_values],
        1,
    )
    temporal_out = call(
        functools.partial(temporal_blend_kernel, blocks),
        "temporal_blend",
        out_shape,
        [],
        [temporal_weights, temporal_inverse, *temporal_values],
        1,
    )
    return (spatial_out, temporal_out)


def solution(mesh):
    placed = P(("video", "tm"), "space", None, None)
    return jax.shard_map(
        on_device,
        mesh=mesh,
        in_specs=(placed,) * 6 + (P(),),
        out_specs=(placed, placed),
        check_vma=False,
    )
```

```python
import functools
import math

import jax
import jax.numpy as jnp
from jax import lax
from jax.experimental import pallas as pl
from jax.experimental.pallas import tpu as pltpu
from jax.sharding import PartitionSpec as P

HEAD_DIM = 72
PAIR = 2 * HEAD_DIM
LANES = 128
WINDOW = 2 * LANES
SCALE = HEAD_DIM ** (-0.5) * math.log2(math.e)
big_negative = -1e30
AXES = ("video", "space", "tm")


def partner_of(index, distance, parity):
    upward = (index // distance) % 2 == parity
    if isinstance(index, int):
        return index + distance if upward else index - distance
    return jnp.where(upward, index + distance, index - distance)


def exchanged(value, distance, parity):
    videos, length, others = [lax.axis_size(axis) for axis in AXES]
    pairs = []
    for video in range(videos):
        for index in range(length):
            there, partner = video, partner_of(index, distance, parity)
            if not 0 <= partner < length:
                partner = index
                there = video ^ 1 if (video ^ 1) < videos else video
            for other in range(others):
                pairs.append(
                    (
                        (video * length + index) * others + other,
                        (there * length + partner) * others + other,
                    )
                )
    return lax.ppermute(value, AXES, pairs)


def swapped(value, axis, step):
    return lax.ppermute(value, axis, [(i, i ^ step) for i in range(lax.axis_size(axis))])


def head_masks(pair, rows):
    lane = lax.broadcasted_iota(jnp.int32, (rows, WINDOW), 1)
    first = (PAIR - LANES) * pair
    return [
        (lane >= first + head * HEAD_DIM) & (lane < first + (head + 1) * HEAD_DIM)
        for head in range(2)
    ]


def window_of(pair):
    return slice(pair * LANES, pair * LANES + WINDOW)


def weigh_pair(pair, queries, keyset, bias):
    rows = queries.shape[0]
    masks = head_masks(pair, rows)
    stacked = jnp.concatenate(
        [queries * mask.astype(jnp.bfloat16) for mask in masks], axis=0
    )
    scores = lax.dot_general(
        stacked, keyset, (((1,), (1,)), ((), ())), preferred_element_type=jnp.float32
    )
    scores = scores * SCALE + bias
    highest = jnp.max(scores, axis=-1, keepdims=True)
    weights = jnp.exp2(scores - highest)
    inverse = 1.0 / jnp.sum(weights, axis=-1, keepdims=True)
    inverse = jnp.where(masks[0], inverse[:rows], jnp.where(masks[1], inverse[rows:], 0.0))
    return weights.astype(jnp.bfloat16), inverse


def blend_pairs(pairs, read_weights, read_inverse, read_values, write):
    carry = None
    for pair in range(pairs):
        inverse = read_inverse(pair)
        rows = inverse.shape[0]
        blended = jnp.dot(
            read_weights(pair), read_values(window_of(pair)), preferred_element_type=jnp.float32
        )
        mask = head_masks(pair, rows)[0]
        both = jnp.where(mask, blended[:rows], blended[rows:]) * inverse
        low = both[:, :LANES]
        if carry is not None:
            low = low + carry
        write(slice(pair * LANES, (pair + 1) * LANES), low.astype(jnp.bfloat16))
        carry = both[:, LANES:]
    write(slice(pairs * LANES, (pairs + 1) * LANES), carry.astype(jnp.bfloat16))


def read_tokens(refs, frame, lanes):
    return jnp.concatenate(
        [ref[frame, :, :, lanes].reshape(-1, WINDOW) for ref in refs], axis=0
    )


def read_row(refs, row, lanes):
    return jnp.concatenate([ref[:, row, :, lanes].reshape(-1, WINDOW) for ref in refs], axis=0)


def stage_kernel(blocks, space, index_ref, lists_ref, *refs):
    count = (len(refs) - 2) // 2
    sources, bias_ref, copies, sems = refs[:count], refs[count], refs[count + 1 : -1], refs[-1]
    moves = [
        pltpu.make_async_copy(source, copy, sems.at[i])
        for i, (source, copy) in enumerate(zip(sources, copies))
    ]
    for move in moves:
        move.start()
    _, rows, columns, _ = sources[0].shape
    index = index_ref[0]
    key_rows = []
    for distance in range(blocks // 2 + 1):
        for parity in range(2 if distance else 1):
            owner = partner_of(index, distance, parity) if distance else index
            first = jnp.where((owner >= 0) & (owner < space), owner * rows, -(2**20))
            row = lax.broadcasted_iota(jnp.int32, (columns, rows * columns), 1) // columns
            key_rows.append(row + first)
    key_rows = jnp.concatenate(key_rows, axis=1)
    for row in range(rows):
        query_row = index * rows + row
        member = key_rows == query_row
        for entry in range(lists_ref.shape[0]):
            member = member | (key_rows == lists_ref[entry, query_row])
        bias = jnp.where(member & (key_rows >= 0), 0.0, big_negative)
        bias_ref[row * columns : (row + 1) * columns] = bias
    for move in moves:
        move.wait()


def staged(arrays, index, lists, blocks, space):
    _, rows, columns, _ = arrays[0].shape
    in_vmem = pl.BlockSpec(memory_space=pltpu.VMEM)
    bias = jax.ShapeDtypeStruct((rows * columns, blocks * rows * columns), jnp.float32)
    return pl.pallas_call(
        functools.partial(stage_kernel, blocks, space),
        out_shape=(bias, *[jax.ShapeDtypeStruct(a.shape, a.dtype) for a in arrays]),
        in_specs=[pl.BlockSpec(memory_space=pltpu.SMEM)] * 2
        + [pl.BlockSpec(memory_space=pl.ANY)] * len(arrays),
        out_specs=(in_vmem,) * (1 + len(arrays)),
        scratch_shapes=[pltpu.SemaphoreType.DMA((len(arrays),))],
        compiler_params=pltpu.CompilerParams(vmem_limit_bytes=40 * 1024 * 1024),
        cost_estimate=pl.CostEstimate(flops=1, bytes_accessed=1, transcendentals=0),
        name="stage",
    )(index, lists, *arrays)


def spatial_weigh_kernel(blocks, bias_ref, q_ref, *refs):
    k_refs, weights_ref, inverse_ref = refs[:blocks], *refs[-2:]
    frames, rows, columns, channels = q_ref.shape
    bias = bias_ref[...]
    bias = jnp.concatenate([bias, bias], axis=0)
    for frame in range(frames):
        for pair in range(channels // PAIR):
            lanes = window_of(pair)
            weights_ref[frame, pair], inverse_ref[frame, pair] = weigh_pair(
                pair, read_tokens([q_ref], frame, lanes), read_tokens(k_refs, frame, lanes), bias
            )


def spatial_blend_kernel(blocks, weights_ref, inverse_ref, *refs):
    v_refs, out_ref = refs[:blocks], refs[blocks]
    frames, rows, columns, channels = out_ref.shape
    for frame in range(frames):

        def write(lanes, value):
            out_ref[frame, :, :, lanes] = value.reshape(rows, columns, LANES)

        blend_pairs(
            channels // PAIR,
            lambda pair: weights_ref[frame, pair],
            lambda pair: inverse_ref[frame, pair],
            lambda lanes: read_tokens(v_refs, frame, lanes),
            write,
        )


def temporal_weigh_kernel(blocks, q_ref, *refs):
    k_refs, weights_ref, inverse_ref = refs[:blocks], *refs[-2:]
    frames, rows, columns, channels = q_ref.shape
    shape = (2 * frames * columns, sum(ref.shape[0] for ref in k_refs) * columns)
    own = lax.broadcasted_iota(jnp.int32, shape, 0) % columns
    other = lax.broadcasted_iota(jnp.int32, shape, 1) % columns
    bias = jnp.where(own == other, 0.0, big_negative)
    for row in range(rows):
        for pair in range(channels // PAIR):
            lanes = window_of(pair)
            weights_ref[row, pair], inverse_ref[row, pair] = weigh_pair(
                pair, read_row([q_ref], row, lanes), read_row(k_refs, row, lanes), bias
            )


def temporal_blend_kernel(blocks, weights_ref, inverse_ref, *refs):
    v_refs, out_ref = refs[:blocks], refs[blocks]
    frames, rows, columns, channels = out_ref.shape
    for row in range(rows):

        def write(lanes, value):
            out_ref[:, row, :, lanes] = value.reshape(frames, columns, LANES)

        blend_pairs(
            channels // PAIR,
            lambda pair: weights_ref[row, pair],
            lambda pair: inverse_ref[row, pair],
            lambda lanes: read_row(v_refs, row, lanes),
            write,
        )


def call(kernel, name, out_shape, scalars, arrays, flops, others=()):
    in_vmem = pl.BlockSpec(memory_space=pltpu.VMEM)
    in_smem = pl.BlockSpec(memory_space=pltpu.SMEM)
    anywhere = pl.BlockSpec(memory_space=pl.ANY)
    return pl.pallas_call(
        kernel,
        out_shape=out_shape,
        in_specs=[in_smem] * len(scalars) + [in_vmem] * len(arrays) + [anywhere] * len(others),
        out_specs=jax.tree.map(lambda _: in_vmem, out_shape),
        compiler_params=pltpu.CompilerParams(vmem_limit_bytes=40 * 1024 * 1024),
        cost_estimate=pl.CostEstimate(
            flops=flops, bytes_accessed=1, transcendentals=0
        ),
        name=name,
    )(*scalars, *arrays, *others)


def join_kernel(count, *refs):
    out_ref = refs[-1]
    first = 0
    for ref in refs[:count]:
        out_ref[first : first + ref.shape[0]] = ref[...]
        first += ref.shape[0]


def joined(arrays, others):
    shape = (sum(a.shape[0] for a in arrays),) + arrays[0].shape[1:]
    return call(
        functools.partial(join_kernel, len(arrays)),
        "join",
        jax.ShapeDtypeStruct(shape, arrays[0].dtype),
        [],
        arrays,
        1,
        others,
    )


def weigh_shapes(groups, channels, queries, keys):
    pairs = channels // PAIR
    return (
        jax.ShapeDtypeStruct((groups, pairs, 2 * queries, keys), jnp.bfloat16),
        jax.ShapeDtypeStruct((groups, pairs, queries, WINDOW), jnp.float32),
    )


def on_device(spatial_q, spatial_k, spatial_v, temporal_q, temporal_k, temporal_v, key_lists):
    frames, rows, columns, channels = spatial_q.shape
    space = lax.axis_size("space")
    reach = -(-(key_lists.shape[1] // 2) // rows)
    index = lax.axis_index("space").reshape(1)
    out_shape = jax.ShapeDtypeStruct(spatial_q.shape, jnp.bfloat16)
    tokens = frames * rows * columns
    first_step = lax.axis_size("tm") // 2

    exchanges = [(d, parity) for d in range(1, reach + 1) for parity in range(2)]
    blocks = 1 + len(exchanges)
    bias, own_q, own_k, own_tv = staged(
        [spatial_q, spatial_k, temporal_v], index, key_lists.T, blocks, space
    )

    def gathered(own, received, others):
        held, step = [own, received], first_step // 2
        while step:
            held = [joined(held, others)]
            held.append(swapped(held[0], "tm", step))
            step //= 2
        return held

    received_keys = swapped(temporal_k, "tm", first_step)
    received_values = swapped(own_tv, "tm", first_step)
    spatial_keys = [own_k] + [exchanged(spatial_k, *which) for which in exchanges]
    spatial_values = [spatial_v] + [
        exchanged(spatial_v, *which) for which in exchanges
    ]

    keys = blocks * rows * columns
    spatial_weights, spatial_inverse = call(
        functools.partial(spatial_weigh_kernel, blocks),
        "spatial_weigh",
        weigh_shapes(frames, channels, rows * columns, keys),
        [],
        [bias, own_q, *spatial_keys],
        1,
        [received_keys],
    )
    temporal_keys = gathered(temporal_k, received_keys, [spatial_weights])
    blocks = len(temporal_keys)
    keys = sum(k.shape[0] for k in temporal_keys) * columns
    temporal_weights, temporal_inverse = call(
        functools.partial(temporal_weigh_kernel, blocks),
        "temporal_weigh",
        weigh_shapes(rows, channels, frames * columns, keys),
        [],
        [temporal_q, *temporal_keys],
        1,
    )
    temporal_values = gathered(own_tv, received_values, [spatial_weights, *spatial_values[1:]])
    spatial_out = call(
        functools.partial(spatial_blend_kernel, len(spatial_values)),
        "spatial_blend",
        out_shape,
        [],
        [spatial_weights, spatial_inverse, *spatial_values],
        1,
    )
    temporal_out = call(
        functools.partial(temporal_blend_kernel, blocks),
        "temporal_blend",
        out_shape,
        [],
        [temporal_weights, temporal_inverse, *temporal_values],
        1,
    )
    return (spatial_out, temporal_out)


def solution(mesh):
    placed = P(("video", "tm"), "space", None, None)
    return jax.shard_map(
        on_device,
        mesh=mesh,
        in_specs=(placed,) * 6 + (P(),),
        out_specs=(placed, placed),
        check_vma=False,
    )
```

```python
import functools
import math

import jax
import jax.numpy as jnp
from jax import lax
from jax.experimental import pallas as pl
from jax.experimental.pallas import tpu as pltpu
from jax.sharding import PartitionSpec as P

HEAD_DIM = 72
PAIR = 2 * HEAD_DIM
LANES = 128
WINDOW = 2 * LANES
SCALE = HEAD_DIM ** (-0.5) * math.log2(math.e)
big_negative = -1e30
AXES = ("video", "space", "tm")


def partner_of(index, distance, parity):
    upward = (index // distance) % 2 == parity
    if isinstance(index, int):
        return index + distance if upward else index - distance
    return jnp.where(upward, index + distance, index - distance)


def exchanged(value, distance, parity):
    videos, length, others = [lax.axis_size(axis) for axis in AXES]
    pairs = []
    for video in range(videos):
        for index in range(length):
            there, partner = video, partner_of(index, distance, parity)
            if not 0 <= partner < length:
                partner = index
                there = video ^ 1 if (video ^ 1) < videos else video
            for other in range(others):
                pairs.append(
                    (
                        (video * length + index) * others + other,
                        (there * length + partner) * others + other,
                    )
                )
    return lax.ppermute(value, AXES, pairs)


def swapped(value, axis, step):
    return lax.ppermute(value, axis, [(i, i ^ step) for i in range(lax.axis_size(axis))])


def head_masks(pair, rows):
    lane = lax.broadcasted_iota(jnp.int32, (rows, WINDOW), 1)
    first = (PAIR - LANES) * pair
    return [
        (lane >= first + head * HEAD_DIM) & (lane < first + (head + 1) * HEAD_DIM)
        for head in range(2)
    ]


def window_of(pair):
    return slice(pair * LANES, pair * LANES + WINDOW)


def weigh_pair(pair, queries, keyset, bias):
    rows = queries.shape[0]
    masks = head_masks(pair, rows)
    stacked = jnp.concatenate(
        [queries * mask.astype(jnp.bfloat16) for mask in masks], axis=0
    )
    scores = lax.dot_general(
        stacked, keyset, (((1,), (1,)), ((), ())), preferred_element_type=jnp.float32
    )
    scores = scores * SCALE + bias
    highest = jnp.max(scores, axis=-1, keepdims=True)
    weights = jnp.exp2(scores - highest)
    inverse = 1.0 / jnp.sum(weights, axis=-1, keepdims=True)
    inverse = jnp.where(masks[0], inverse[:rows], jnp.where(masks[1], inverse[rows:], 0.0))
    return weights.astype(jnp.bfloat16), inverse


def blend_pairs(pairs, read_weights, read_inverse, read_values, write):
    carry = None
    for pair in range(pairs):
        inverse = read_inverse(pair)
        rows = inverse.shape[0]
        blended = jnp.dot(
            read_weights(pair), read_values(window_of(pair)), preferred_element_type=jnp.float32
        )
        mask = head_masks(pair, rows)[0]
        both = jnp.where(mask, blended[:rows], blended[rows:]) * inverse
        low = both[:, :LANES]
        if carry is not None:
            low = low + carry
        write(slice(pair * LANES, (pair + 1) * LANES), low.astype(jnp.bfloat16))
        carry = both[:, LANES:]
    write(slice(pairs * LANES, (pairs + 1) * LANES), carry.astype(jnp.bfloat16))


def read_tokens(refs, frame, lanes):
    return jnp.concatenate(
        [ref[frame, :, :, lanes].reshape(-1, WINDOW) for ref in refs], axis=0
    )


def read_row(refs, row, lanes):
    return jnp.concatenate([ref[:, row, :, lanes].reshape(-1, WINDOW) for ref in refs], axis=0)


def stage_kernel(blocks, space, index_ref, lists_ref, *refs):
    count = (len(refs) - 2) // 2
    sources, bias_ref, copies, sems = refs[:count], refs[count], refs[count + 1 : -1], refs[-1]
    moves = [
        pltpu.make_async_copy(source, copy, sems.at[i])
        for i, (source, copy) in enumerate(zip(sources, copies))
    ]
    for move in moves:
        move.start()
    _, rows, columns, _ = sources[0].shape
    index = index_ref[0]
    key_rows = []
    for distance in range(blocks // 2 + 1):
        for parity in (1, 0) if distance else (0,):
            owner = partner_of(index, distance, parity) if distance else index
            first = jnp.where((owner >= 0) & (owner < space), owner * rows, -(2**20))
            row = lax.broadcasted_iota(jnp.int32, (columns, rows * columns), 1) // columns
            key_rows.append(row + first)
    key_rows = jnp.concatenate(key_rows, axis=1)
    for row in range(rows):
        query_row = index * rows + row
        member = key_rows == query_row
        for entry in range(lists_ref.shape[0]):
            member = member | (key_rows == lists_ref[entry, query_row])
        bias = jnp.where(member & (key_rows >= 0), 0.0, big_negative)
        bias_ref[row * columns : (row + 1) * columns] = bias
    for move in moves:
        move.wait()


def staged(arrays, index, lists, blocks, space):
    _, rows, columns, _ = arrays[0].shape
    in_vmem = pl.BlockSpec(memory_space=pltpu.VMEM)
    bias = jax.ShapeDtypeStruct((rows * columns, blocks * rows * columns), jnp.float32)
    return pl.pallas_call(
        functools.partial(stage_kernel, blocks, space),
        out_shape=(bias, *[jax.ShapeDtypeStruct(a.shape, a.dtype) for a in arrays]),
        in_specs=[pl.BlockSpec(memory_space=pltpu.SMEM)] * 2
        + [pl.BlockSpec(memory_space=pl.ANY)] * len(arrays),
        out_specs=(in_vmem,) * (1 + len(arrays)),
        scratch_shapes=[pltpu.SemaphoreType.DMA((len(arrays),))],
        compiler_params=pltpu.CompilerParams(vmem_limit_bytes=53 * 1024 * 1024),
        cost_estimate=pl.CostEstimate(flops=1, bytes_accessed=1, transcendentals=0),
        name="stage",
    )(index, lists, *arrays)


def spatial_weigh_kernel(blocks, bias_ref, q_ref, *refs):
    k_refs, weights_ref, inverse_ref = refs[:blocks], *refs[-2:]
    frames, rows, columns, channels = q_ref.shape
    bias = bias_ref[...]
    bias = jnp.concatenate([bias, bias], axis=0)
    for frame in range(frames):
        for pair in range(channels // PAIR):
            lanes = window_of(pair)
            weights_ref[frame, pair], inverse_ref[frame, pair] = weigh_pair(
                pair, read_tokens([q_ref], frame, lanes), read_tokens(k_refs, frame, lanes), bias
            )


def spatial_blend_kernel(blocks, weights_ref, inverse_ref, *refs):
    v_refs, out_ref = refs[:blocks], refs[blocks]
    frames, rows, columns, channels = out_ref.shape
    for frame in range(frames):

        def write(lanes, value):
            out_ref[frame, :, :, lanes] = value.reshape(rows, columns, LANES)

        blend_pairs(
            channels // PAIR,
            lambda pair: weights_ref[frame, pair],
            lambda pair: inverse_ref[frame, pair],
            lambda lanes: read_tokens(v_refs, frame, lanes),
            write,
        )


def temporal_weigh_kernel(blocks, q_ref, *refs):
    k_refs, weights_ref, inverse_ref = refs[:blocks], *refs[-2:]
    frames, rows, columns, channels = q_ref.shape
    shape = (2 * frames * columns, sum(ref.shape[0] for ref in k_refs) * columns)
    own = lax.broadcasted_iota(jnp.int32, shape, 0) % columns
    other = lax.broadcasted_iota(jnp.int32, shape, 1) % columns
    bias = jnp.where(own == other, 0.0, big_negative)
    for row in range(rows):
        for pair in range(channels // PAIR):
            lanes = window_of(pair)
            weights_ref[row, pair], inverse_ref[row, pair] = weigh_pair(
                pair, read_row([q_ref], row, lanes), read_row(k_refs, row, lanes), bias
            )


def temporal_blend_kernel(blocks, weights_ref, inverse_ref, *refs):
    v_refs, out_ref = refs[:blocks], refs[blocks]
    frames, rows, columns, channels = out_ref.shape
    for row in range(rows):

        def write(lanes, value):
            out_ref[:, row, :, lanes] = value.reshape(frames, columns, LANES)

        blend_pairs(
            channels // PAIR,
            lambda pair: weights_ref[row, pair],
            lambda pair: inverse_ref[row, pair],
            lambda lanes: read_row(v_refs, row, lanes),
            write,
        )


def call(kernel, name, out_shape, scalars, arrays, flops, others=()):
    in_vmem = pl.BlockSpec(memory_space=pltpu.VMEM)
    in_smem = pl.BlockSpec(memory_space=pltpu.SMEM)
    anywhere = pl.BlockSpec(memory_space=pl.ANY)
    return pl.pallas_call(
        kernel,
        out_shape=out_shape,
        in_specs=[in_smem] * len(scalars) + [in_vmem] * len(arrays) + [anywhere] * len(others),
        out_specs=jax.tree.map(lambda _: in_vmem, out_shape),
        compiler_params=pltpu.CompilerParams(vmem_limit_bytes=40 * 1024 * 1024),
        cost_estimate=pl.CostEstimate(
            flops=flops, bytes_accessed=1, transcendentals=0
        ),
        name=name,
    )(*scalars, *arrays, *others)


def join_kernel(count, *refs):
    out_ref = refs[-1]
    first = 0
    for ref in refs[:count]:
        out_ref[first : first + ref.shape[0]] = ref[...]
        first += ref.shape[0]


def joined(arrays, others):
    shape = (sum(a.shape[0] for a in arrays),) + arrays[0].shape[1:]
    return call(
        functools.partial(join_kernel, len(arrays)),
        "join",
        jax.ShapeDtypeStruct(shape, arrays[0].dtype),
        [],
        arrays,
        1,
        others,
    )


def weigh_shapes(groups, channels, queries, keys):
    pairs = channels // PAIR
    return (
        jax.ShapeDtypeStruct((groups, pairs, 2 * queries, keys), jnp.bfloat16),
        jax.ShapeDtypeStruct((groups, pairs, queries, WINDOW), jnp.float32),
    )


def on_device(spatial_q, spatial_k, spatial_v, temporal_q, temporal_k, temporal_v, key_lists):
    frames, rows, columns, channels = spatial_q.shape
    space = lax.axis_size("space")
    reach = -(-(key_lists.shape[1] // 2) // rows)
    index = lax.axis_index("space").reshape(1)
    out_shape = jax.ShapeDtypeStruct(spatial_q.shape, jnp.bfloat16)
    tokens = frames * rows * columns
    first_step = lax.axis_size("tm") // 2

    exchanges = [(d, parity) for d in range(1, reach + 1) for parity in (1, 0)]
    blocks = 1 + len(exchanges)
    bias, own_q, own_k, own_tv = staged(
        [spatial_q, spatial_k, temporal_v], index, key_lists.T, blocks, space
    )

    def gathered(own, received, others):
        held, step = [own, received], first_step // 2
        while step:
            held = [joined(held, others)]
            held.append(swapped(held[0], "tm", step))
            step //= 2
        return held

    received_keys = swapped(temporal_k, "tm", first_step)
    received_values = swapped(own_tv, "tm", first_step)
    spatial_keys = [own_k] + [exchanged(spatial_k, *which) for which in exchanges]
    spatial_values = [spatial_v] + [
        exchanged(spatial_v, *which) for which in exchanges
    ]

    keys = blocks * rows * columns
    spatial_weights, spatial_inverse = call(
        functools.partial(spatial_weigh_kernel, blocks),
        "spatial_weigh",
        weigh_shapes(frames, channels, rows * columns, keys),
        [],
        [bias, own_q, *spatial_keys],
        1,
        [received_keys],
    )
    temporal_keys = gathered(temporal_k, received_keys, [spatial_weights])
    blocks = len(temporal_keys)
    keys = sum(k.shape[0] for k in temporal_keys) * columns
    temporal_weights, temporal_inverse = call(
        functools.partial(temporal_weigh_kernel, blocks),
        "temporal_weigh",
        weigh_shapes(rows, channels, frames * columns, keys),
        [],
        [temporal_q, *temporal_keys],
        1,
    )
    temporal_values = gathered(own_tv, received_values, [spatial_weights, *spatial_values[1:]])
    spatial_out = call(
        functools.partial(spatial_blend_kernel, len(spatial_values)),
        "spatial_blend",
        out_shape,
        [],
        [spatial_weights, spatial_inverse, *spatial_values],
        1,
    )
    temporal_out = call(
        functools.partial(temporal_blend_kernel, blocks),
        "temporal_blend",
        out_shape,
        [],
        [temporal_weights, temporal_inverse, *temporal_values],
        1,
    )
    return (spatial_out, temporal_out)


def solution(mesh):
    placed = P(("video", "tm"), "space", None, None)
    return jax.shard_map(
        on_device,
        mesh=mesh,
        in_specs=(placed,) * 6 + (P(),),
        out_specs=(placed, placed),
        check_vma=False,
    )
```

```python
import functools
import math

import jax
import jax.numpy as jnp
from jax import lax
from jax.experimental import pallas as pl
from jax.experimental.pallas import tpu as pltpu
from jax.sharding import PartitionSpec as P

HEAD_DIM = 72
PAIR = 2 * HEAD_DIM
LANES = 128
WINDOW = 2 * LANES
SCALE = HEAD_DIM ** (-0.5) * math.log2(math.e)
big_negative = -1e30
AXES = ("video", "space", "tm")


def partner_of(index, distance, parity):
    upward = (index // distance) % 2 == parity
    if isinstance(index, int):
        return index + distance if upward else index - distance
    return jnp.where(upward, index + distance, index - distance)


def exchanged(value, distance, parity):
    videos, length, others = [lax.axis_size(axis) for axis in AXES]
    pairs = []
    for video in range(videos):
        for index in range(length):
            there, partner = video, partner_of(index, distance, parity)
            if not 0 <= partner < length:
                partner = index
                there = video ^ 1 if (video ^ 1) < videos else video
            for other in range(others):
                pairs.append(
                    (
                        (video * length + index) * others + other,
                        (there * length + partner) * others + other,
                    )
                )
    return lax.ppermute(value, AXES, pairs)


def swapped(value, axis, step):
    return lax.ppermute(value, axis, [(i, i ^ step) for i in range(lax.axis_size(axis))])


def head_masks(pair, rows):
    lane = lax.broadcasted_iota(jnp.int32, (rows, WINDOW), 1)
    first = (PAIR - LANES) * pair
    return [
        (lane >= first + head * HEAD_DIM) & (lane < first + (head + 1) * HEAD_DIM)
        for head in range(2)
    ]


def window_of(pair):
    return slice(pair * LANES, pair * LANES + WINDOW)


def weigh_pair(pair, queries, keyset, bias):
    rows = queries.shape[0]
    masks = head_masks(pair, rows)
    stacked = jnp.concatenate(
        [queries * mask.astype(jnp.bfloat16) for mask in masks], axis=0
    )
    scores = lax.dot_general(
        stacked, keyset, (((1,), (1,)), ((), ())), preferred_element_type=jnp.float32
    )
    scores = scores * SCALE + bias
    highest = jnp.max(scores, axis=-1, keepdims=True)
    weights = jnp.exp2(scores - highest)
    inverse = 1.0 / jnp.sum(weights, axis=-1, keepdims=True)
    inverse = jnp.where(masks[0], inverse[:rows], jnp.where(masks[1], inverse[rows:], 0.0))
    return weights.astype(jnp.bfloat16), inverse


def blend_pairs(pairs, read_weights, read_inverse, read_values, write):
    carry = None
    for pair in range(pairs):
        inverse = read_inverse(pair)
        rows = inverse.shape[0]
        blended = jnp.dot(
            read_weights(pair), read_values(window_of(pair)), preferred_element_type=jnp.float32
        )
        mask = head_masks(pair, rows)[0]
        both = jnp.where(mask, blended[:rows], blended[rows:]) * inverse
        low = both[:, :LANES]
        if carry is not None:
            low = low + carry
        write(slice(pair * LANES, (pair + 1) * LANES), low.astype(jnp.bfloat16))
        carry = both[:, LANES:]
    write(slice(pairs * LANES, (pairs + 1) * LANES), carry.astype(jnp.bfloat16))


def read_tokens(refs, frame, lanes):
    return jnp.concatenate(
        [ref[frame, :, :, lanes].reshape(-1, WINDOW) for ref in refs], axis=0
    )


def read_row(refs, row, lanes):
    return jnp.concatenate([ref[:, row, :, lanes].reshape(-1, WINDOW) for ref in refs], axis=0)


def stage_kernel(blocks, space, index_ref, lists_ref, *refs):
    count = (len(refs) - 2) // 2
    sources, bias_ref, copies, sems = refs[:count], refs[count], refs[count + 1 : -1], refs[-1]
    moves = [
        pltpu.make_async_copy(source, copy, sems.at[i])
        for i, (source, copy) in enumerate(zip(sources, copies))
    ]
    for move in moves:
        move.start()
    _, rows, columns, _ = sources[0].shape
    index = index_ref[0]
    key_rows = []
    for distance in range(blocks // 2 + 1):
        for parity in (1, 0) if distance else (0,):
            owner = partner_of(index, distance, parity) if distance else index
            first = jnp.where((owner >= 0) & (owner < space), owner * rows, -(2**20))
            row = lax.broadcasted_iota(jnp.int32, (columns, rows * columns), 1) // columns
            key_rows.append(row + first)
    key_rows = jnp.concatenate(key_rows, axis=1)
    for row in range(rows):
        query_row = index * rows + row
        member = key_rows == query_row
        for entry in range(lists_ref.shape[0]):
            member = member | (key_rows == lists_ref[entry, query_row])
        bias = jnp.where(member & (key_rows >= 0), 0.0, big_negative)
        bias_ref[row * columns : (row + 1) * columns] = bias
    for move in moves:
        move.wait()


def staged(arrays, index, lists, blocks, space):
    _, rows, columns, _ = arrays[0].shape
    in_vmem = pl.BlockSpec(memory_space=pltpu.VMEM)
    bias = jax.ShapeDtypeStruct((rows * columns, blocks * rows * columns), jnp.float32)
    return pl.pallas_call(
        functools.partial(stage_kernel, blocks, space),
        out_shape=(bias, *[jax.ShapeDtypeStruct(a.shape, a.dtype) for a in arrays]),
        in_specs=[pl.BlockSpec(memory_space=pltpu.SMEM)] * 2
        + [pl.BlockSpec(memory_space=pl.ANY)] * len(arrays),
        out_specs=(in_vmem,) * (1 + len(arrays)),
        scratch_shapes=[pltpu.SemaphoreType.DMA((len(arrays),))],
        compiler_params=pltpu.CompilerParams(vmem_limit_bytes=53 * 1024 * 1024),
        cost_estimate=pl.CostEstimate(flops=1, bytes_accessed=1, transcendentals=0),
        name="stage",
    )(index, lists, *arrays)


def spatial_weigh_kernel(blocks, bias_ref, q_ref, *refs):
    k_refs, weights_ref, inverse_ref = refs[:blocks], *refs[-2:]
    frames, rows, columns, channels = q_ref.shape
    bias = bias_ref[...]
    bias = jnp.concatenate([bias, bias], axis=0)
    for frame in range(frames):
        for pair in range(channels // PAIR):
            lanes = window_of(pair)
            weights_ref[frame, pair], inverse_ref[frame, pair] = weigh_pair(
                pair, read_tokens([q_ref], frame, lanes), read_tokens(k_refs, frame, lanes), bias
            )


def spatial_blend_kernel(blocks, weights_ref, inverse_ref, *refs):
    v_refs, (out_ref, held, sems) = refs[:blocks], refs[-3:]
    frames, rows, columns, channels = held.shape
    pairs = channels // PAIR
    moves = []
    for frame in range(frames):
        sent = 0

        def write(lanes, value):
            nonlocal sent
            held[frame, :, :, lanes] = value.reshape(rows, columns, LANES)
            if lanes.stop in (channels // 2 // LANES * LANES, channels):
                part = (frame, slice(None), slice(None), slice(sent, lanes.stop))
                moves.append(
                    pltpu.make_async_copy(held.at[part], out_ref.at[part], sems.at[len(moves)])
                )
                moves[-1].start()
                sent = lanes.stop

        blend_pairs(
            pairs,
            lambda pair: weights_ref[frame, pair],
            lambda pair: inverse_ref[frame, pair],
            lambda lanes: read_tokens(v_refs, frame, lanes),
            write,
        )
    for move in moves:
        move.wait()


def temporal_weigh_kernel(blocks, q_ref, *refs):
    k_refs, weights_ref, inverse_ref = refs[:blocks], *refs[-2:]
    frames, rows, columns, channels = q_ref.shape
    shape = (2 * frames * columns, sum(ref.shape[0] for ref in k_refs) * columns)
    own = lax.broadcasted_iota(jnp.int32, shape, 0) % columns
    other = lax.broadcasted_iota(jnp.int32, shape, 1) % columns
    bias = jnp.where(own == other, 0.0, big_negative)
    for row in range(rows):
        for pair in range(channels // PAIR):
            lanes = window_of(pair)
            weights_ref[row, pair], inverse_ref[row, pair] = weigh_pair(
                pair, read_row([q_ref], row, lanes), read_row(k_refs, row, lanes), bias
            )


def temporal_blend_kernel(blocks, weights_ref, inverse_ref, *refs):
    v_refs, (out_ref, held, sems) = refs[:blocks], refs[-3:]
    frames, rows, columns, channels = held.shape
    moves = []
    for row in range(rows):

        def write(lanes, value):
            held[:, row, :, lanes] = value.reshape(frames, columns, LANES)

        blend_pairs(
            channels // PAIR,
            lambda pair: weights_ref[row, pair],
            lambda pair: inverse_ref[row, pair],
            lambda lanes: read_row(v_refs, row, lanes),
            write,
        )
        moves.append(
            pltpu.make_async_copy(held.at[:, row], out_ref.at[:, row], sems.at[row])
        )
        moves[-1].start()
    for move in moves:
        move.wait()


def call(kernel, name, out_shape, scalars, arrays, flops, others=(), parts=0):
    in_vmem = pl.BlockSpec(memory_space=pltpu.VMEM)
    in_smem = pl.BlockSpec(memory_space=pltpu.SMEM)
    anywhere = pl.BlockSpec(memory_space=pl.ANY)
    return pl.pallas_call(
        kernel,
        out_shape=out_shape,
        in_specs=[in_smem] * len(scalars) + [in_vmem] * len(arrays) + [anywhere] * len(others),
        out_specs=jax.tree.map(lambda _: anywhere if parts else in_vmem, out_shape),
        scratch_shapes=[
            pltpu.VMEM(out_shape.shape, out_shape.dtype),
            pltpu.SemaphoreType.DMA((parts,)),
        ]
        if parts
        else [],
        compiler_params=pltpu.CompilerParams(vmem_limit_bytes=40 * 1024 * 1024),
        cost_estimate=pl.CostEstimate(
            flops=flops, bytes_accessed=1, transcendentals=0
        ),
        name=name,
    )(*scalars, *arrays, *others)


def join_kernel(count, *refs):
    out_ref = refs[-1]
    first = 0
    for ref in refs[:count]:
        out_ref[first : first + ref.shape[0]] = ref[...]
        first += ref.shape[0]


def joined(arrays, others):
    shape = (sum(a.shape[0] for a in arrays),) + arrays[0].shape[1:]
    return call(
        functools.partial(join_kernel, len(arrays)),
        "join",
        jax.ShapeDtypeStruct(shape, arrays[0].dtype),
        [],
        arrays,
        1,
        others,
    )


def weigh_shapes(groups, channels, queries, keys):
    pairs = channels // PAIR
    return (
        jax.ShapeDtypeStruct((groups, pairs, 2 * queries, keys), jnp.bfloat16),
        jax.ShapeDtypeStruct((groups, pairs, queries, WINDOW), jnp.float32),
    )


def on_device(spatial_q, spatial_k, spatial_v, temporal_q, temporal_k, temporal_v, key_lists):
    frames, rows, columns, channels = spatial_q.shape
    space = lax.axis_size("space")
    reach = -(-(key_lists.shape[1] // 2) // rows)
    index = lax.axis_index("space").reshape(1)
    out_shape = jax.ShapeDtypeStruct(spatial_q.shape, jnp.bfloat16)
    tokens = frames * rows * columns
    first_step = lax.axis_size("tm") // 2

    exchanges = [(d, parity) for d in range(1, reach + 1) for parity in (1, 0)]
    blocks = 1 + len(exchanges)
    bias, own_q, own_k, own_tv = staged(
        [spatial_q, spatial_k, temporal_v], index, key_lists.T, blocks, space
    )

    def gathered(own, received, others):
        held, step = [own, received], first_step // 2
        while step:
            held = [joined(held, others)]
            held.append(swapped(held[0], "tm", step))
            step //= 2
        return held

    received_keys = swapped(temporal_k, "tm", first_step)
    received_values = swapped(own_tv, "tm", first_step)
    spatial_keys = [own_k] + [exchanged(spatial_k, *which) for which in exchanges]
    spatial_values = [spatial_v] + [
        exchanged(spatial_v, *which) for which in exchanges
    ]

    keys = blocks * rows * columns
    spatial_weights, spatial_inverse = call(
        functools.partial(spatial_weigh_kernel, blocks),
        "spatial_weigh",
        weigh_shapes(frames, channels, rows * columns, keys),
        [],
        [bias, own_q, *spatial_keys],
        1,
        [received_keys],
    )
    temporal_keys = gathered(temporal_k, received_keys, [spatial_weights])
    blocks = len(temporal_keys)
    keys = sum(k.shape[0] for k in temporal_keys) * columns
    temporal_weights, temporal_inverse = call(
        functools.partial(temporal_weigh_kernel, blocks),
        "temporal_weigh",
        weigh_shapes(rows, channels, frames * columns, keys),
        [],
        [temporal_q, *temporal_keys],
        1,
    )
    temporal_values = gathered(own_tv, received_values, [spatial_weights, *spatial_values[1:]])
    spatial_out = call(
        functools.partial(spatial_blend_kernel, len(spatial_values)),
        "spatial_blend",
        out_shape,
        [],
        [spatial_weights, spatial_inverse, *spatial_values],
        1,
        parts=2 * frames,
    )
    temporal_out = call(
        functools.partial(temporal_blend_kernel, blocks),
        "temporal_blend",
        out_shape,
        [],
        [temporal_weights, temporal_inverse, *temporal_values],
        1,
        parts=rows,
    )
    return (spatial_out, temporal_out)


def solution(mesh):
    placed = P(("video", "tm"), "space", None, None)
    return jax.shard_map(
        on_device,
        mesh=mesh,
        in_specs=(placed,) * 6 + (P(),),
        out_specs=(placed, placed),
        check_vma=False,
    )
```

```python
import functools
import math

import jax
import jax.numpy as jnp
from jax import lax
from jax.experimental import pallas as pl
from jax.experimental.pallas import tpu as pltpu
from jax.sharding import PartitionSpec as P

HEAD_DIM = 72
PAIR = 2 * HEAD_DIM
LANES = 128
WINDOW = 2 * LANES
SCALE = HEAD_DIM ** (-0.5) * math.log2(math.e)
big_negative = -1e30
AXES = ("video", "space", "tm")


def partner_of(index, distance, parity):
    upward = (index // distance) % 2 == parity
    if isinstance(index, int):
        return index + distance if upward else index - distance
    return jnp.where(upward, index + distance, index - distance)


def exchanged(value, distance, parity):
    videos, length, others = [lax.axis_size(axis) for axis in AXES]
    pairs = []
    for video in range(videos):
        for index in range(length):
            there, partner = video, partner_of(index, distance, parity)
            if not 0 <= partner < length:
                partner = index
                there = video ^ 1 if (video ^ 1) < videos else video
            for other in range(others):
                pairs.append(
                    (
                        (video * length + index) * others + other,
                        (there * length + partner) * others + other,
                    )
                )
    return lax.ppermute(value, AXES, pairs)


def swapped(value, axis, step):
    return lax.ppermute(value, axis, [(i, i ^ step) for i in range(lax.axis_size(axis))])


def head_masks(pair, rows):
    lane = lax.broadcasted_iota(jnp.int32, (rows, WINDOW), 1)
    first = (PAIR - LANES) * pair
    return [
        (lane >= first + head * HEAD_DIM) & (lane < first + (head + 1) * HEAD_DIM)
        for head in range(2)
    ]


def window_of(pair):
    return slice(pair * LANES, pair * LANES + WINDOW)


def weigh_pair(pair, queries, keyset, bias):
    rows = queries.shape[0]
    masks = head_masks(pair, rows)
    stacked = jnp.concatenate(
        [queries * mask.astype(jnp.bfloat16) for mask in masks], axis=0
    )
    scores = lax.dot_general(
        stacked, keyset, (((1,), (1,)), ((), ())), preferred_element_type=jnp.float32
    )
    scores = scores * SCALE + bias
    highest = jnp.max(scores, axis=-1, keepdims=True)
    weights = jnp.exp2(scores - highest)
    inverse = 1.0 / jnp.sum(weights, axis=-1, keepdims=True)
    inverse = jnp.where(masks[0], inverse[:rows], jnp.where(masks[1], inverse[rows:], 0.0))
    return weights.astype(jnp.bfloat16), inverse


def blend_pairs(pairs, read_weights, read_inverse, read_values, write):
    carry = None
    for pair in range(pairs):
        inverse = read_inverse(pair)
        rows = inverse.shape[0]
        blended = jnp.dot(
            read_weights(pair), read_values(window_of(pair)), preferred_element_type=jnp.float32
        )
        mask = head_masks(pair, rows)[0]
        both = jnp.where(mask, blended[:rows], blended[rows:]) * inverse
        low = both[:, :LANES]
        if carry is not None:
            low = low + carry
        write(slice(pair * LANES, (pair + 1) * LANES), low.astype(jnp.bfloat16))
        carry = both[:, LANES:]
    write(slice(pairs * LANES, (pairs + 1) * LANES), carry.astype(jnp.bfloat16))


def read_tokens(refs, frame, lanes):
    return jnp.concatenate(
        [ref[frame, :, :, lanes].reshape(-1, WINDOW) for ref in refs], axis=0
    )


def read_row(refs, row, lanes):
    return jnp.concatenate([ref[:, row, :, lanes].reshape(-1, WINDOW) for ref in refs], axis=0)


def stage_kernel(blocks, space, index_ref, lists_ref, *refs):
    count = (len(refs) - 2) // 2
    sources, bias_ref, copies, sems = refs[:count], refs[count], refs[count + 1 : -1], refs[-1]
    moves = [
        pltpu.make_async_copy(source, copy, sems.at[i])
        for i, (source, copy) in enumerate(zip(sources, copies))
    ]
    for move in moves:
        move.start()
    _, rows, columns, _ = sources[0].shape
    index = index_ref[0]
    key_rows = []
    for distance in range(blocks // 2 + 1):
        for parity in (0, 1) if distance else (0,):
            owner = partner_of(index, distance, parity) if distance else index
            first = jnp.where((owner >= 0) & (owner < space), owner * rows, -(2**20))
            row = lax.broadcasted_iota(jnp.int32, (columns, rows * columns), 1) // columns
            key_rows.append(row + first)
    key_rows = jnp.concatenate(key_rows, axis=1)
    for row in range(rows):
        query_row = index * rows + row
        member = key_rows == query_row
        for entry in range(lists_ref.shape[0]):
            member = member | (key_rows == lists_ref[entry, query_row])
        bias = jnp.where(member & (key_rows >= 0), 0.0, big_negative)
        bias_ref[row * columns : (row + 1) * columns] = bias
    for move in moves:
        move.wait()


def staged(arrays, index, lists, blocks, space):
    _, rows, columns, _ = arrays[0].shape
    in_vmem = pl.BlockSpec(memory_space=pltpu.VMEM)
    bias = jax.ShapeDtypeStruct((rows * columns, blocks * rows * columns), jnp.float32)
    return pl.pallas_call(
        functools.partial(stage_kernel, blocks, space),
        out_shape=(bias, *[jax.ShapeDtypeStruct(a.shape, a.dtype) for a in arrays]),
        in_specs=[pl.BlockSpec(memory_space=pltpu.SMEM)] * 2
        + [pl.BlockSpec(memory_space=pl.ANY)] * len(arrays),
        out_specs=(in_vmem,) * (1 + len(arrays)),
        scratch_shapes=[pltpu.SemaphoreType.DMA((len(arrays),))],
        compiler_params=pltpu.CompilerParams(vmem_limit_bytes=53 * 1024 * 1024),
        cost_estimate=pl.CostEstimate(flops=1, bytes_accessed=1, transcendentals=0),
        name="stage",
    )(index, lists, *arrays)


def spatial_weigh_kernel(blocks, bias_ref, q_ref, *refs):
    k_refs, weights_ref, inverse_ref = refs[:blocks], *refs[-2:]
    frames, rows, columns, channels = q_ref.shape
    bias = bias_ref[...]
    bias = jnp.concatenate([bias, bias], axis=0)
    for frame in range(frames):
        for pair in range(channels // PAIR):
            lanes = window_of(pair)
            weights_ref[frame, pair], inverse_ref[frame, pair] = weigh_pair(
                pair, read_tokens([q_ref], frame, lanes), read_tokens(k_refs, frame, lanes), bias
            )


def spatial_blend_kernel(blocks, weights_ref, inverse_ref, *refs):
    v_refs, (out_ref, held, sems) = refs[:blocks], refs[-3:]
    frames, rows, columns, channels = held.shape
    pairs = channels // PAIR
    moves = []
    for frame in range(frames):
        sent = 0

        def write(lanes, value):
            nonlocal sent
            held[frame, :, :, lanes] = value.reshape(rows, columns, LANES)
            if lanes.stop in (channels // 2 // LANES * LANES, channels):
                part = (frame, slice(None), slice(None), slice(sent, lanes.stop))
                moves.append(
                    pltpu.make_async_copy(held.at[part], out_ref.at[part], sems.at[len(moves)])
                )
                moves[-1].start()
                sent = lanes.stop

        blend_pairs(
            pairs,
            lambda pair: weights_ref[frame, pair],
            lambda pair: inverse_ref[frame, pair],
            lambda lanes: read_tokens(v_refs, frame, lanes),
            write,
        )
    for move in moves:
        move.wait()


def temporal_weigh_kernel(blocks, q_ref, *refs):
    k_refs, weights_ref, inverse_ref = refs[:blocks], *refs[-2:]
    frames, rows, columns, channels = q_ref.shape
    shape = (2 * frames * columns, sum(ref.shape[0] for ref in k_refs) * columns)
    own = lax.broadcasted_iota(jnp.int32, shape, 0) % columns
    other = lax.broadcasted_iota(jnp.int32, shape, 1) % columns
    bias = jnp.where(own == other, 0.0, big_negative)
    for row in range(rows):
        for pair in range(channels // PAIR):
            lanes = window_of(pair)
            weights_ref[row, pair], inverse_ref[row, pair] = weigh_pair(
                pair, read_row([q_ref], row, lanes), read_row(k_refs, row, lanes), bias
            )


def temporal_blend_kernel(blocks, weights_ref, inverse_ref, *refs):
    v_refs, (out_ref, held, sems) = refs[:blocks], refs[-3:]
    frames, rows, columns, channels = held.shape
    moves = []
    for row in range(rows):

        def write(lanes, value):
            held[:, row, :, lanes] = value.reshape(frames, columns, LANES)

        blend_pairs(
            channels // PAIR,
            lambda pair: weights_ref[row, pair],
            lambda pair: inverse_ref[row, pair],
            lambda lanes: read_row(v_refs, row, lanes),
            write,
        )
        moves.append(
            pltpu.make_async_copy(held.at[:, row], out_ref.at[:, row], sems.at[row])
        )
        moves[-1].start()
    for move in moves:
        move.wait()


def call(kernel, name, out_shape, scalars, arrays, flops, others=(), parts=0):
    in_vmem = pl.BlockSpec(memory_space=pltpu.VMEM)
    in_smem = pl.BlockSpec(memory_space=pltpu.SMEM)
    anywhere = pl.BlockSpec(memory_space=pl.ANY)
    return pl.pallas_call(
        kernel,
        out_shape=out_shape,
        in_specs=[in_smem] * len(scalars) + [in_vmem] * len(arrays) + [anywhere] * len(others),
        out_specs=jax.tree.map(lambda _: anywhere if parts else in_vmem, out_shape),
        scratch_shapes=[
            pltpu.VMEM(out_shape.shape, out_shape.dtype),
            pltpu.SemaphoreType.DMA((parts,)),
        ]
        if parts
        else [],
        compiler_params=pltpu.CompilerParams(vmem_limit_bytes=40 * 1024 * 1024),
        cost_estimate=pl.CostEstimate(
            flops=flops, bytes_accessed=1, transcendentals=0
        ),
        name=name,
    )(*scalars, *arrays, *others)


def join_kernel(count, *refs):
    out_ref = refs[-1]
    first = 0
    for ref in refs[:count]:
        out_ref[first : first + ref.shape[0]] = ref[...]
        first += ref.shape[0]


def joined(arrays, others):
    shape = (sum(a.shape[0] for a in arrays),) + arrays[0].shape[1:]
    return call(
        functools.partial(join_kernel, len(arrays)),
        "join",
        jax.ShapeDtypeStruct(shape, arrays[0].dtype),
        [],
        arrays,
        1,
        others,
    )


def weigh_shapes(groups, channels, queries, keys):
    pairs = channels // PAIR
    return (
        jax.ShapeDtypeStruct((groups, pairs, 2 * queries, keys), jnp.bfloat16),
        jax.ShapeDtypeStruct((groups, pairs, queries, WINDOW), jnp.float32),
    )


def on_device(spatial_q, spatial_k, spatial_v, temporal_q, temporal_k, temporal_v, key_lists):
    frames, rows, columns, channels = spatial_q.shape
    space = lax.axis_size("space")
    reach = -(-(key_lists.shape[1] // 2) // rows)
    index = lax.axis_index("space").reshape(1)
    out_shape = jax.ShapeDtypeStruct(spatial_q.shape, jnp.bfloat16)
    tokens = frames * rows * columns
    first_step = lax.axis_size("tm") // 2

    exchanges = [(d, parity) for d in range(1, reach + 1) for parity in (0, 1)]
    blocks = 1 + len(exchanges)
    bias, own_q, own_k, own_tv = staged(
        [spatial_q, spatial_k, temporal_v], index, key_lists.T, blocks, space
    )

    def gathered(held, step):
        other = swapped(held, "tm", step)
        if step == 1:
            return [held, other]
        return gathered(joined([held, other], []), step // 2)

    received_keys = swapped(temporal_k, "tm", first_step)
    received_values = swapped(own_tv, "tm", first_step)
    spatial_keys = [own_k] + [exchanged(spatial_k, *which) for which in exchanges]
    spatial_values = [spatial_v] + [
        exchanged(spatial_v, *which) for which in exchanges
    ]

    keys = blocks * rows * columns
    joined_keys = joined([temporal_k, received_keys], [])
    spatial_weights, spatial_inverse = call(
        functools.partial(spatial_weigh_kernel, blocks),
        "spatial_weigh",
        weigh_shapes(frames, channels, rows * columns, keys),
        [],
        [bias, own_q, *spatial_keys],
        1,
        [joined_keys],
    )
    def weigh_all(queries, keyset, before):
        keysets = gathered(keyset, first_step // 2)
        keys = sum(k.shape[0] for k in keysets) * columns
        return call(
            functools.partial(temporal_weigh_kernel, len(keysets)),
            "temporal_weigh",
            weigh_shapes(rows, channels, frames * columns, keys),
            [],
            [queries, *keysets],
            1,
            [before],
        )

    def weigh_none(queries, keyset, before):
        keys = lax.axis_size("tm") * frames * columns
        shapes = weigh_shapes(rows, channels, frames * columns, keys)
        return tuple(jnp.zeros(shape.shape, shape.dtype) for shape in shapes)

    temporal_weights, temporal_inverse = lax.cond(
        lax.axis_index("tm") >= 0,
        weigh_all,
        weigh_none,
        temporal_q,
        joined_keys,
        spatial_weights,
    )
    temporal_values = gathered(joined([own_tv, received_values], [temporal_weights]), first_step // 2)
    spatial_out = call(
        functools.partial(spatial_blend_kernel, len(spatial_values)),
        "spatial_blend",
        out_shape,
        [],
        [spatial_weights, spatial_inverse, *spatial_values],
        10**10,
        parts=2 * frames,
    )
    temporal_out = call(
        functools.partial(temporal_blend_kernel, len(temporal_values)),
        "temporal_blend",
        out_shape,
        [],
        [temporal_weights, temporal_inverse, *temporal_values],
        1,
        parts=rows,
    )
    return (spatial_out, temporal_out)


def solution(mesh):
    placed = P(("video", "tm"), "space", None, None)
    return jax.shard_map(
        on_device,
        mesh=mesh,
        in_specs=(placed,) * 6 + (P(),),
        out_specs=(placed, placed),
        check_vma=False,
    )
```

```python
import functools
import math

import jax
import jax.numpy as jnp
from jax import lax
from jax.experimental import pallas as pl
from jax.experimental.pallas import tpu as pltpu
from jax.sharding import PartitionSpec as P

HEAD_DIM = 72
PAIR = 2 * HEAD_DIM
LANES = 128
WINDOW = 2 * LANES
SCALE = HEAD_DIM ** (-0.5) * math.log2(math.e)
big_negative = -1e30
AXES = ("video", "space", "tm")


def partner_of(index, distance, parity):
    upward = (index // distance) % 2 == parity
    if isinstance(index, int):
        return index + distance if upward else index - distance
    return jnp.where(upward, index + distance, index - distance)


def exchanged(value, distance, parity):
    videos, length, others = [lax.axis_size(axis) for axis in AXES]
    pairs = []
    for video in range(videos):
        for index in range(length):
            there, partner = video, partner_of(index, distance, parity)
            if not 0 <= partner < length:
                partner = index
                there = video ^ 1 if (video ^ 1) < videos else video
            for other in range(others):
                pairs.append(
                    (
                        (video * length + index) * others + other,
                        (there * length + partner) * others + other,
                    )
                )
    return lax.ppermute(value, AXES, pairs)


def swapped(value, axis, step):
    return lax.ppermute(value, axis, [(i, i ^ step) for i in range(lax.axis_size(axis))])


def head_masks(pair, rows):
    lane = lax.broadcasted_iota(jnp.int32, (rows, WINDOW), 1)
    first = (PAIR - LANES) * pair
    return [
        (lane >= first + head * HEAD_DIM) & (lane < first + (head + 1) * HEAD_DIM)
        for head in range(2)
    ]


def window_of(pair):
    return slice(pair * LANES, pair * LANES + WINDOW)


def weigh_pair(pair, queries, keyset, bias):
    rows = queries.shape[0]
    masks = head_masks(pair, rows)
    stacked = jnp.concatenate(
        [queries * mask.astype(jnp.bfloat16) for mask in masks], axis=0
    )
    scores = lax.dot_general(
        stacked, keyset, (((1,), (1,)), ((), ())), preferred_element_type=jnp.float32
    )
    scores = scores * SCALE + bias
    highest = jnp.max(scores, axis=-1, keepdims=True)
    weights = jnp.exp2(scores - highest)
    inverse = 1.0 / jnp.sum(weights, axis=-1, keepdims=True)
    inverse = jnp.where(masks[0], inverse[:rows], jnp.where(masks[1], inverse[rows:], 0.0))
    return weights.astype(jnp.bfloat16), inverse


def blend_pairs(pairs, read_weights, read_inverse, read_values, write):
    carry = None
    for pair in range(pairs):
        inverse = read_inverse(pair)
        rows = inverse.shape[0]
        blended = jnp.dot(
            read_weights(pair), read_values(window_of(pair)), preferred_element_type=jnp.float32
        )
        mask = head_masks(pair, rows)[0]
        both = jnp.where(mask, blended[:rows], blended[rows:]) * inverse
        low = both[:, :LANES]
        if carry is not None:
            low = low + carry
        write(slice(pair * LANES, (pair + 1) * LANES), low.astype(jnp.bfloat16))
        carry = both[:, LANES:]
    write(slice(pairs * LANES, (pairs + 1) * LANES), carry.astype(jnp.bfloat16))


def read_tokens(refs, frame, lanes):
    return jnp.concatenate(
        [ref[frame, :, :, lanes].reshape(-1, WINDOW) for ref in refs], axis=0
    )


def read_row(refs, row, lanes):
    return jnp.concatenate([ref[:, row, :, lanes].reshape(-1, WINDOW) for ref in refs], axis=0)


def stage_kernel(blocks, space, index_ref, lists_ref, *refs):
    count = (len(refs) - 2) // 2
    sources, bias_ref, copies, sems = refs[:count], refs[count], refs[count + 1 : -1], refs[-1]
    moves = [
        pltpu.make_async_copy(source, copy, sems.at[i])
        for i, (source, copy) in enumerate(zip(sources, copies))
    ]
    for move in moves:
        move.start()
    _, rows, columns, _ = sources[0].shape
    index = index_ref[0]
    key_rows = []
    for distance in range(blocks // 2 + 1):
        for parity in (0, 1) if distance else (0,):
            owner = partner_of(index, distance, parity) if distance else index
            first = jnp.where((owner >= 0) & (owner < space), owner * rows, -(2**20))
            row = lax.broadcasted_iota(jnp.int32, (columns, rows * columns), 1) // columns
            key_rows.append(row + first)
    key_rows = jnp.concatenate(key_rows, axis=1)
    for row in range(rows):
        query_row = index * rows + row
        member = key_rows == query_row
        for entry in range(lists_ref.shape[0]):
            member = member | (key_rows == lists_ref[entry, query_row])
        bias = jnp.where(member & (key_rows >= 0), 0.0, big_negative)
        bias_ref[row * columns : (row + 1) * columns] = bias
    for move in moves:
        move.wait()


def staged(arrays, index, lists, blocks, space):
    _, rows, columns, _ = arrays[0].shape
    in_vmem = pl.BlockSpec(memory_space=pltpu.VMEM)
    bias = jax.ShapeDtypeStruct((rows * columns, blocks * rows * columns), jnp.float32)
    return pl.pallas_call(
        functools.partial(stage_kernel, blocks, space),
        out_shape=(bias, *[jax.ShapeDtypeStruct(a.shape, a.dtype) for a in arrays]),
        in_specs=[pl.BlockSpec(memory_space=pltpu.SMEM)] * 2
        + [pl.BlockSpec(memory_space=pl.ANY)] * len(arrays),
        out_specs=(in_vmem,) * (1 + len(arrays)),
        scratch_shapes=[pltpu.SemaphoreType.DMA((len(arrays),))],
        compiler_params=pltpu.CompilerParams(vmem_limit_bytes=53568 * 1024),
        cost_estimate=pl.CostEstimate(flops=1, bytes_accessed=1, transcendentals=0),
        name="stage",
    )(index, lists, *arrays)


def spatial_weigh_kernel(blocks, bias_ref, q_ref, *refs):
    k_refs, weights_ref, inverse_ref, token_ref = refs[:blocks], *refs[-3:]
    frames, rows, columns, channels = q_ref.shape
    token_ref[...] = jnp.zeros(token_ref.shape, token_ref.dtype)
    bias = bias_ref[...]
    bias = jnp.concatenate([bias, bias], axis=0)
    for frame in range(frames):
        for pair in range(channels // PAIR):
            lanes = window_of(pair)
            weights_ref[frame, pair], inverse_ref[frame, pair] = weigh_pair(
                pair, read_tokens([q_ref], frame, lanes), read_tokens(k_refs, frame, lanes), bias
            )


def spatial_blend_kernel(blocks, weights_ref, inverse_ref, *refs):
    v_refs, (out_ref, held, sems) = refs[:blocks], refs[-3:]
    frames, rows, columns, channels = held.shape
    pairs = channels // PAIR
    moves = []
    for frame in range(frames):
        sent = 0

        def write(lanes, value):
            nonlocal sent
            held[frame, :, :, lanes] = value.reshape(rows, columns, LANES)
            if lanes.stop in (channels // 2 // LANES * LANES, channels):
                part = (frame, slice(None), slice(None), slice(sent, lanes.stop))
                moves.append(
                    pltpu.make_async_copy(held.at[part], out_ref.at[part], sems.at[len(moves)])
                )
                moves[-1].start()
                sent = lanes.stop

        blend_pairs(
            pairs,
            lambda pair: weights_ref[frame, pair],
            lambda pair: inverse_ref[frame, pair],
            lambda lanes: read_tokens(v_refs, frame, lanes),
            write,
        )
    for move in moves:
        move.wait()


def temporal_weigh_kernel(blocks, q_ref, *refs):
    k_refs, weights_ref, inverse_ref = refs[:blocks], *refs[-2:]
    frames, rows, columns, channels = q_ref.shape
    shape = (2 * frames * columns, sum(ref.shape[0] for ref in k_refs) * columns)
    own = lax.broadcasted_iota(jnp.int32, shape, 0) % columns
    other = lax.broadcasted_iota(jnp.int32, shape, 1) % columns
    bias = jnp.where(own == other, 0.0, big_negative)
    for row in range(rows):
        for pair in range(channels // PAIR):
            lanes = window_of(pair)
            weights_ref[row, pair], inverse_ref[row, pair] = weigh_pair(
                pair, read_row([q_ref], row, lanes), read_row(k_refs, row, lanes), bias
            )


def temporal_blend_kernel(blocks, weights_ref, inverse_ref, *refs):
    v_refs, (out_ref, held, sems) = refs[:blocks], refs[-3:]
    frames, rows, columns, channels = held.shape
    moves = []
    for row in range(rows):

        def write(lanes, value):
            held[:, row, :, lanes] = value.reshape(frames, columns, LANES)

        blend_pairs(
            channels // PAIR,
            lambda pair: weights_ref[row, pair],
            lambda pair: inverse_ref[row, pair],
            lambda lanes: read_row(v_refs, row, lanes),
            write,
        )
        moves.append(
            pltpu.make_async_copy(held.at[:, row], out_ref.at[:, row], sems.at[row])
        )
        moves[-1].start()
    for move in moves:
        move.wait()


def call(kernel, name, out_shape, scalars, arrays, flops, others=(), parts=0):
    in_vmem = pl.BlockSpec(memory_space=pltpu.VMEM)
    in_smem = pl.BlockSpec(memory_space=pltpu.SMEM)
    anywhere = pl.BlockSpec(memory_space=pl.ANY)
    return pl.pallas_call(
        kernel,
        out_shape=out_shape,
        in_specs=[in_smem] * len(scalars) + [in_vmem] * len(arrays) + [anywhere] * len(others),
        out_specs=jax.tree.map(lambda _: anywhere if parts else in_vmem, out_shape),
        scratch_shapes=[
            pltpu.VMEM(out_shape.shape, out_shape.dtype),
            pltpu.SemaphoreType.DMA((parts,)),
        ]
        if parts
        else [],
        compiler_params=pltpu.CompilerParams(vmem_limit_bytes=40 * 1024 * 1024),
        cost_estimate=pl.CostEstimate(
            flops=flops, bytes_accessed=1, transcendentals=0
        ),
        name=name,
    )(*scalars, *arrays, *others)


def join_kernel(count, *refs):
    out_ref = refs[-1]
    first = 0
    for ref in refs[:count]:
        out_ref[first : first + ref.shape[0]] = ref[...]
        first += ref.shape[0]


def joined(arrays, others):
    shape = (sum(a.shape[0] for a in arrays),) + arrays[0].shape[1:]
    return call(
        functools.partial(join_kernel, len(arrays)),
        "join",
        jax.ShapeDtypeStruct(shape, arrays[0].dtype),
        [],
        arrays,
        1,
        others,
    )


def weigh_shapes(groups, channels, queries, keys):
    pairs = channels // PAIR
    return (
        jax.ShapeDtypeStruct((groups, pairs, 2 * queries, keys), jnp.bfloat16),
        jax.ShapeDtypeStruct((groups, pairs, queries, WINDOW), jnp.float32),
    )


def on_device(spatial_q, spatial_k, spatial_v, temporal_q, temporal_k, temporal_v, key_lists):
    frames, rows, columns, channels = spatial_q.shape
    space = lax.axis_size("space")
    reach = -(-(key_lists.shape[1] // 2) // rows)
    index = lax.axis_index("space").reshape(1)
    out_shape = jax.ShapeDtypeStruct(spatial_q.shape, jnp.bfloat16)
    tokens = frames * rows * columns
    first_step = lax.axis_size("tm") // 2

    exchanges = [(d, parity) for d in range(1, reach + 1) for parity in (0, 1)]
    blocks = 1 + len(exchanges)
    bias, own_sq, own_sk, own_sv, own_tq, own_tk, own_tv = staged(
        [spatial_q, spatial_k, spatial_v, temporal_q, temporal_k, temporal_v],
        index,
        key_lists.T,
        blocks,
        space,
    )

    def gathered(held, step):
        other = swapped(held, "tm", step)
        if step == 1:
            return [held, other]
        return gathered(joined([held, other], []), step // 2)

    received_keys = swapped(temporal_k, "tm", first_step)
    received_values = swapped(own_tv, "tm", first_step)
    spatial_keys = [own_sk] + [exchanged(spatial_k, *which) for which in exchanges]
    spatial_values = [own_sv] + [exchanged(own_sv, *which) for which in exchanges]

    keys = blocks * rows * columns
    joined_keys = joined([own_tk, received_keys], [])
    spatial_weights, spatial_inverse, token = call(
        functools.partial(spatial_weigh_kernel, blocks),
        "spatial_weigh",
        weigh_shapes(frames, channels, rows * columns, keys)
        + (jax.ShapeDtypeStruct((8, LANES), jnp.float32),),
        [],
        [bias, own_sq, *spatial_keys],
        1,
        [joined_keys],
    )
    def weigh_all(queries, keyset, before):
        keysets = gathered(keyset, first_step // 2)
        keys = sum(k.shape[0] for k in keysets) * columns
        return call(
            functools.partial(temporal_weigh_kernel, len(keysets)),
            "temporal_weigh",
            weigh_shapes(rows, channels, frames * columns, keys),
            [],
            [queries, *keysets],
            1,
            [before],
        )

    def weigh_none(queries, keyset, before):
        keys = lax.axis_size("tm") * frames * columns
        shapes = weigh_shapes(rows, channels, frames * columns, keys)
        return tuple(jnp.zeros(shape.shape, shape.dtype) for shape in shapes)

    temporal_weights, temporal_inverse = lax.cond(
        lax.axis_index("tm") >= 0,
        weigh_all,
        weigh_none,
        own_tq,
        joined_keys,
        token,
    )
    temporal_values = gathered(joined([own_tv, received_values], [temporal_weights]), first_step // 2)
    spatial_out = call(
        functools.partial(spatial_blend_kernel, len(spatial_values)),
        "spatial_blend",
        out_shape,
        [],
        [spatial_weights, spatial_inverse, *spatial_values],
        10**10,
        parts=2 * frames,
    )
    temporal_out = call(
        functools.partial(temporal_blend_kernel, len(temporal_values)),
        "temporal_blend",
        out_shape,
        [],
        [temporal_weights, temporal_inverse, *temporal_values],
        1,
        parts=rows,
    )
    return (spatial_out, temporal_out)


def solution(mesh):
    placed = P(("video", "tm"), "space", None, None)
    return jax.shard_map(
        on_device,
        mesh=mesh,
        in_specs=(placed,) * 6 + (P(),),
        out_specs=(placed, placed),
        check_vma=False,
    )
```

```python
import functools
import math

import jax
import jax.numpy as jnp
from jax import lax
from jax.experimental import pallas as pl
from jax.experimental.pallas import tpu as pltpu
from jax.sharding import PartitionSpec as P

HEAD_DIM = 72
LANES = 128
WINDOW = 2 * LANES
SCALE = HEAD_DIM ** (-0.5) * math.log2(math.e)
big_negative = -1e30
AXES = ("video", "space", "tm")


def partner_of(index, distance, parity):
    upward = (index // distance) % 2 == parity
    if isinstance(index, int):
        return index + distance if upward else index - distance
    return jnp.where(upward, index + distance, index - distance)


def exchanged(value, distance, parity):
    videos, length, others = [lax.axis_size(axis) for axis in AXES]
    pairs = []
    for video in range(videos):
        for index in range(length):
            there, partner = video, partner_of(index, distance, parity)
            if not 0 <= partner < length:
                partner = index
                there = video ^ 1 if (video ^ 1) < videos else video
            for other in range(others):
                pairs.append(
                    (
                        (video * length + index) * others + other,
                        (there * length + partner) * others + other,
                    )
                )
    return lax.ppermute(value, AXES, pairs)


def swapped(value, axis, step):
    return lax.ppermute(value, axis, [(i, i ^ step) for i in range(lax.axis_size(axis))])


def windows_of(channels):
    windows = []
    for first in range(0, channels, WINDOW):
        last = min(first + WINDOW, channels)
        windows.append((slice(first, last), range(first // HEAD_DIM, (last - 1) // HEAD_DIM + 1)))
    return windows


def by_head(parts, heads, first, rows):
    lane = lax.broadcasted_iota(jnp.int32, (rows, LANES), 1) + first
    chosen = parts[0]
    for head, part in zip(heads[1:], parts[1:]):
        chosen = jnp.where(lane >= head * HEAD_DIM, part, chosen)
    return chosen


def tile_heads(first):
    return range(first // HEAD_DIM, (first + LANES - 1) // HEAD_DIM + 1)


def weigh(channels, read_queries, read_keys, bias, write_weights, write_inverse):
    scores, inverses = {}, {}
    rows = bias.shape[0]
    for lanes, heads in windows_of(channels):
        queries = read_queries(lanes)
        lane = lax.broadcasted_iota(jnp.int32, queries.shape, 1) + lanes.start
        stacked = []
        for head in heads:
            mask = (lane >= head * HEAD_DIM) & (lane < (head + 1) * HEAD_DIM)
            stacked.append(queries * mask.astype(jnp.bfloat16))
        both = lax.dot_general(
            jnp.concatenate(stacked, axis=0),
            read_keys(lanes),
            (((1,), (1,)), ((), ())),
            preferred_element_type=jnp.float32,
        )
        for place, head in enumerate(heads):
            part = both[place * rows : (place + 1) * rows]
            scores[head] = scores[head] + part if head in scores else part
            if (head + 1) * HEAD_DIM > lanes.stop:
                continue
            masked = scores.pop(head) * SCALE + bias
            highest = jnp.max(masked, axis=-1, keepdims=True)
            weights = jnp.exp2(masked - highest)
            inverses[head] = 1.0 / jnp.sum(weights, axis=-1, keepdims=True)
            write_weights(head, weights.astype(jnp.bfloat16))
    for first in range(0, channels, LANES):
        heads = tile_heads(first)
        parts = [jnp.broadcast_to(inverses[head], (rows, LANES)) for head in heads]
        write_inverse(slice(first, first + LANES), by_head(parts, heads, first, rows))


def blend(channels, rows, read_weights, read_inverse, read_values, write):
    for lanes, heads in windows_of(channels):
        blended = jnp.dot(
            read_weights(heads), read_values(lanes), preferred_element_type=jnp.float32
        )
        for first in range(lanes.start, lanes.stop, LANES):
            tile = slice(first, first + LANES)
            inside = slice(first - lanes.start, first - lanes.start + LANES)
            parts = []
            for head in tile_heads(first):
                place = (head - heads[0]) * rows
                parts.append(blended[place : place + rows, inside])
            chosen = by_head(parts, tile_heads(first), first, rows) * read_inverse(tile)
            write(tile, chosen.astype(jnp.bfloat16))


def read_tokens(refs, frame, lanes):
    return jnp.concatenate(
        [ref[frame, :, :, lanes].reshape(-1, lanes.stop - lanes.start) for ref in refs], axis=0
    )


def read_row(refs, row, lanes):
    return jnp.concatenate(
        [ref[:, row, :, lanes].reshape(-1, lanes.stop - lanes.start) for ref in refs], axis=0
    )


def stage_kernel(blocks, space, index_ref, lists_ref, *refs):
    count = (len(refs) - 2) // 2
    sources, bias_ref, copies, sems = refs[:count], refs[count], refs[count + 1 : -1], refs[-1]
    moves = [
        pltpu.make_async_copy(source, copy, sems.at[i])
        for i, (source, copy) in enumerate(zip(sources, copies))
    ]
    for move in moves:
        move.start()
    _, rows, columns, _ = sources[0].shape
    index = index_ref[0]
    key_rows = []
    for distance in range(blocks // 2 + 1):
        for parity in (1, 0) if distance else (0,):
            owner = partner_of(index, distance, parity) if distance else index
            first = jnp.where((owner >= 0) & (owner < space), owner * rows, -(2**20))
            row = lax.broadcasted_iota(jnp.int32, (columns, rows * columns), 1) // columns
            key_rows.append(row + first)
    key_rows = jnp.concatenate(key_rows, axis=1)
    for row in range(rows):
        query_row = index * rows + row
        member = key_rows == query_row
        for entry in range(lists_ref.shape[0]):
            member = member | (key_rows == lists_ref[entry, query_row])
        bias = jnp.where(member & (key_rows >= 0), 0.0, big_negative)
        bias_ref[row * columns : (row + 1) * columns] = bias
    for move in moves:
        move.wait()


def staged(arrays, index, lists, blocks, space):
    _, rows, columns, _ = arrays[0].shape
    in_vmem = pl.BlockSpec(memory_space=pltpu.VMEM)
    bias = jax.ShapeDtypeStruct((rows * columns, blocks * rows * columns), jnp.float32)
    return pl.pallas_call(
        functools.partial(stage_kernel, blocks, space),
        out_shape=(bias, *[jax.ShapeDtypeStruct(a.shape, a.dtype) for a in arrays]),
        in_specs=[pl.BlockSpec(memory_space=pltpu.SMEM)] * 2
        + [pl.BlockSpec(memory_space=pl.ANY)] * len(arrays),
        out_specs=(in_vmem,) * (1 + len(arrays)),
        scratch_shapes=[pltpu.SemaphoreType.DMA((len(arrays),))],
        compiler_params=pltpu.CompilerParams(vmem_limit_bytes=53 * 1024 * 1024),
        cost_estimate=pl.CostEstimate(flops=1, bytes_accessed=1, transcendentals=0),
        name="stage",
    )(index, lists, *arrays)


def spatial_weigh_kernel(blocks, bias_ref, q_ref, *refs):
    k_refs, weights_ref, inverse_ref = refs[:blocks], *refs[-2:]
    bias = bias_ref[...]
    for frame in range(q_ref.shape[0]):

        def write_weights(head, value):
            weights_ref[frame, head] = value

        def write_inverse(lanes, value):
            inverse_ref[frame, :, lanes] = value

        weigh(
            q_ref.shape[-1],
            lambda lanes: read_tokens([q_ref], frame, lanes),
            lambda lanes: read_tokens(k_refs, frame, lanes),
            bias,
            write_weights,
            write_inverse,
        )


def read_weights(weights_ref, group, heads):
    _, _, rows, keys = weights_ref.shape
    return weights_ref[group, heads[0] : heads[-1] + 1].reshape(len(heads) * rows, keys)


def spatial_blend_kernel(blocks, weights_ref, inverse_ref, *refs):
    v_refs, (out_ref, held, sems) = refs[:blocks], refs[-3:]
    frames, rows, columns, channels = held.shape
    moves = []
    for frame in range(frames):
        sent = 0

        def write(lanes, value):
            nonlocal sent
            held[frame, :, :, lanes] = value.reshape(rows, columns, LANES)
            if lanes.stop in (channels // 2 // WINDOW * WINDOW, channels):
                part = (frame, slice(None), slice(None), slice(sent, lanes.stop))
                moves.append(
                    pltpu.make_async_copy(held.at[part], out_ref.at[part], sems.at[len(moves)])
                )
                moves[-1].start()
                sent = lanes.stop

        blend(
            channels,
            rows * columns,
            lambda heads: read_weights(weights_ref, frame, heads),
            lambda lanes: inverse_ref[frame, :, lanes],
            lambda lanes: read_tokens(v_refs, frame, lanes),
            write,
        )
    for move in moves:
        move.wait()


def temporal_weigh_kernel(blocks, q_ref, *refs):
    k_refs, weights_ref, inverse_ref = refs[:blocks], *refs[-2:]
    frames, rows, columns, channels = q_ref.shape
    shape = (frames * columns, sum(ref.shape[0] for ref in k_refs) * columns)
    own = lax.broadcasted_iota(jnp.int32, shape, 0) % columns
    other = lax.broadcasted_iota(jnp.int32, shape, 1) % columns
    bias = jnp.where(own == other, 0.0, big_negative)
    for row in range(rows):

        def write_weights(head, value):
            weights_ref[row, head] = value

        def write_inverse(lanes, value):
            inverse_ref[row, :, lanes] = value

        weigh(
            channels,
            lambda lanes: read_row([q_ref], row, lanes),
            lambda lanes: read_row(k_refs, row, lanes),
            bias,
            write_weights,
            write_inverse,
        )


def temporal_blend_kernel(blocks, weights_ref, inverse_ref, *refs):
    v_refs, (out_ref, held, sems) = refs[:blocks], refs[-3:]
    frames, rows, columns, channels = held.shape
    moves = []
    for row in range(rows):

        def write(lanes, value):
            held[:, row, :, lanes] = value.reshape(frames, columns, LANES)

        blend(
            channels,
            frames * columns,
            lambda heads: read_weights(weights_ref, row, heads),
            lambda lanes: inverse_ref[row, :, lanes],
            lambda lanes: read_row(v_refs, row, lanes),
            write,
        )
        moves.append(
            pltpu.make_async_copy(held.at[:, row], out_ref.at[:, row], sems.at[row])
        )
        moves[-1].start()
    for move in moves:
        move.wait()


def call(kernel, name, out_shape, scalars, arrays, flops, others=(), parts=0):
    in_vmem = pl.BlockSpec(memory_space=pltpu.VMEM)
    in_smem = pl.BlockSpec(memory_space=pltpu.SMEM)
    anywhere = pl.BlockSpec(memory_space=pl.ANY)
    return pl.pallas_call(
        kernel,
        out_shape=out_shape,
        in_specs=[in_smem] * len(scalars) + [in_vmem] * len(arrays) + [anywhere] * len(others),
        out_specs=jax.tree.map(lambda _: anywhere if parts else in_vmem, out_shape),
        scratch_shapes=[
            pltpu.VMEM(out_shape.shape, out_shape.dtype),
            pltpu.SemaphoreType.DMA((parts,)),
        ]
        if parts
        else [],
        compiler_params=pltpu.CompilerParams(vmem_limit_bytes=40 * 1024 * 1024),
        cost_estimate=pl.CostEstimate(
            flops=flops, bytes_accessed=1, transcendentals=0
        ),
        name=name,
    )(*scalars, *arrays, *others)


def join_kernel(count, *refs):
    out_ref = refs[-1]
    first = 0
    for ref in refs[:count]:
        out_ref[first : first + ref.shape[0]] = ref[...]
        first += ref.shape[0]


def joined(arrays, others):
    shape = (sum(a.shape[0] for a in arrays),) + arrays[0].shape[1:]
    return call(
        functools.partial(join_kernel, len(arrays)),
        "join",
        jax.ShapeDtypeStruct(shape, arrays[0].dtype),
        [],
        arrays,
        1,
        others,
    )


def weigh_shapes(groups, channels, queries, keys):
    heads = channels // HEAD_DIM
    return (
        jax.ShapeDtypeStruct((groups, heads, queries, keys), jnp.bfloat16),
        jax.ShapeDtypeStruct((groups, queries, channels), jnp.float32),
    )


def on_device(spatial_q, spatial_k, spatial_v, temporal_q, temporal_k, temporal_v, key_lists):
    frames, rows, columns, channels = spatial_q.shape
    space = lax.axis_size("space")
    reach = -(-(key_lists.shape[1] // 2) // rows)
    index = lax.axis_index("space").reshape(1)
    out_shape = jax.ShapeDtypeStruct(spatial_q.shape, jnp.bfloat16)
    tokens = frames * rows * columns
    first_step = lax.axis_size("tm") // 2

    exchanges = [(d, parity) for d in range(1, reach + 1) for parity in (1, 0)]
    blocks = 1 + len(exchanges)
    bias, own_q, own_k, own_tv = staged(
        [spatial_q, spatial_k, temporal_v], index, key_lists.T, blocks, space
    )

    def gathered(own, received, others):
        held, step = [own, received], first_step // 2
        while step:
            held = [joined(held, others)]
            held.append(swapped(held[0], "tm", step))
            step //= 2
        return held

    received_keys = swapped(temporal_k, "tm", first_step)
    received_values = swapped(own_tv, "tm", first_step)
    spatial_keys = [own_k] + [exchanged(spatial_k, *which) for which in exchanges]
    spatial_values = [spatial_v] + [
        exchanged(spatial_v, *which) for which in exchanges
    ]

    keys = blocks * rows * columns
    spatial_weights, spatial_inverse = call(
        functools.partial(spatial_weigh_kernel, blocks),
        "spatial_weigh",
        weigh_shapes(frames, channels, rows * columns, keys),
        [],
        [bias, own_q, *spatial_keys],
        1,
        [received_keys],
    )
    temporal_keys = gathered(temporal_k, received_keys, [spatial_weights])
    blocks = len(temporal_keys)
    keys = sum(k.shape[0] for k in temporal_keys) * columns
    temporal_weights, temporal_inverse = call(
        functools.partial(temporal_weigh_kernel, blocks),
        "temporal_weigh",
        weigh_shapes(rows, channels, frames * columns, keys),
        [],
        [temporal_q, *temporal_keys],
        1,
    )
    temporal_values = gathered(own_tv, received_values, [spatial_weights, *spatial_values[1:]])
    spatial_out = call(
        functools.partial(spatial_blend_kernel, len(spatial_values)),
        "spatial_blend",
        out_shape,
        [],
        [spatial_weights, spatial_inverse, *spatial_values],
        1,
        parts=2 * frames,
    )
    temporal_out = call(
        functools.partial(temporal_blend_kernel, blocks),
        "temporal_blend",
        out_shape,
        [],
        [temporal_weights, temporal_inverse, *temporal_values],
        1,
        parts=rows,
    )
    return (spatial_out, temporal_out)


def solution(mesh):
    placed = P(("video", "tm"), "space", None, None)
    return jax.shard_map(
        on_device,
        mesh=mesh,
        in_specs=(placed,) * 6 + (P(),),
        out_specs=(placed, placed),
        check_vma=False,
    )
```

```python
import functools
import math

import jax
import jax.numpy as jnp
from jax import lax
from jax.experimental import pallas as pl
from jax.experimental.pallas import tpu as pltpu
from jax.sharding import PartitionSpec as P

HEAD_DIM = 72
LANES = 128
WINDOW = 2 * LANES
SCALE = HEAD_DIM ** (-0.5) * math.log2(math.e)
big_negative = -1e30
AXES = ("space", "tm")


def partner_of(index, distance, parity):
    upward = (index // distance) % 2 == parity
    if isinstance(index, int):
        return index + distance if upward else index - distance
    return jnp.where(upward, index + distance, index - distance)


def exchanged(value, distance, parity):
    length, others = [lax.axis_size(axis) for axis in AXES]
    pairs = []
    for index in range(length):
        partner = partner_of(index, distance, parity)
        for other in range(others):
            if 0 <= partner < length:
                target = partner * others + other
            else:
                target = index * others + (other ^ 1 if (other ^ 1) < others else other)
            pairs.append((index * others + other, target))
    return lax.ppermute(value, AXES, pairs)


def swapped(value, axis, step):
    return lax.ppermute(value, axis, [(i, i ^ step) for i in range(lax.axis_size(axis))])


def windows_of(channels):
    windows = []
    for first in range(0, channels, WINDOW):
        last = min(first + WINDOW, channels)
        windows.append((slice(first, last), range(first // HEAD_DIM, (last - 1) // HEAD_DIM + 1)))
    return windows


def by_head(parts, heads, first, rows):
    lane = lax.broadcasted_iota(jnp.int32, (rows, LANES), 1) + first
    chosen = parts[0]
    for head, part in zip(heads[1:], parts[1:]):
        chosen = jnp.where(lane >= head * HEAD_DIM, part, chosen)
    return chosen


def tile_heads(first):
    return range(first // HEAD_DIM, (first + LANES - 1) // HEAD_DIM + 1)


def weigh(channels, read_queries, read_keys, bias, write_weights, write_inverse):
    scores, inverses = {}, {}
    rows = bias.shape[0]
    for lanes, heads in windows_of(channels):
        queries = read_queries(lanes)
        lane = lax.broadcasted_iota(jnp.int32, queries.shape, 1) + lanes.start
        stacked = []
        for head in heads:
            mask = (lane >= head * HEAD_DIM) & (lane < (head + 1) * HEAD_DIM)
            stacked.append(queries * mask.astype(jnp.bfloat16))
        both = lax.dot_general(
            jnp.concatenate(stacked, axis=0),
            read_keys(lanes),
            (((1,), (1,)), ((), ())),
            preferred_element_type=jnp.float32,
        )
        for place, head in enumerate(heads):
            part = both[place * rows : (place + 1) * rows]
            scores[head] = scores[head] + part if head in scores else part
            if (head + 1) * HEAD_DIM > lanes.stop:
                continue
            masked = scores.pop(head) * SCALE + bias
            highest = jnp.max(masked, axis=-1, keepdims=True)
            weights = jnp.exp2(masked - highest)
            inverses[head] = 1.0 / jnp.sum(weights, axis=-1, keepdims=True)
            write_weights(head, weights.astype(jnp.bfloat16))
    for first in range(0, channels, LANES):
        heads = tile_heads(first)
        parts = [jnp.broadcast_to(inverses[head], (rows, LANES)) for head in heads]
        write_inverse(slice(first, first + LANES), by_head(parts, heads, first, rows))


def blend(channels, rows, read_weights, read_inverse, read_values, write):
    blended = []
    for first in range(0, channels, LANES):
        heads = tile_heads(first)
        pair = first // LANES
        if first + WINDOW <= channels:
            values = read_values(slice(first, first + WINDOW))
            weights = read_weights(range(2 * pair, 2 * pair + 2))
            blended.append(jnp.dot(weights, values, preferred_element_type=jnp.float32))
        parts = []
        for head in heads:
            place, lane = head % 2 * rows, first - head // 2 * LANES
            parts.append(blended[head // 2][place : place + rows, lane : lane + LANES])
        tile = slice(first, first + LANES)
        chosen = by_head(parts, heads, first, rows) * read_inverse(tile)
        write(tile, chosen.astype(jnp.bfloat16))


def read_tokens(refs, frame, lanes):
    return jnp.concatenate(
        [ref[frame, :, :, lanes].reshape(-1, lanes.stop - lanes.start) for ref in refs], axis=0
    )


def read_row(refs, row, lanes):
    return jnp.concatenate(
        [ref[:, row, :, lanes].reshape(-1, lanes.stop - lanes.start) for ref in refs], axis=0
    )


def stage_kernel(blocks, space, index_ref, lists_ref, *refs):
    count = (len(refs) - 2) // 2
    sources, bias_ref, copies, sems = refs[:count], refs[count], refs[count + 1 : -1], refs[-1]
    moves = [
        pltpu.make_async_copy(source, copy, sems.at[i])
        for i, (source, copy) in enumerate(zip(sources, copies))
    ]
    for move in moves:
        move.start()
    _, rows, columns, _ = sources[0].shape
    index = index_ref[0]
    key_rows = []
    for distance in range(blocks // 2 + 1):
        for parity in (1, 0) if distance else (0,):
            owner = partner_of(index, distance, parity) if distance else index
            first = jnp.where((owner >= 0) & (owner < space), owner * rows, -(2**20))
            row = lax.broadcasted_iota(jnp.int32, (columns, rows * columns), 1) // columns
            key_rows.append(row + first)
    key_rows = jnp.concatenate(key_rows, axis=1)
    for row in range(rows):
        query_row = index * rows + row
        member = key_rows == query_row
        for entry in range(lists_ref.shape[0]):
            member = member | (key_rows == lists_ref[entry, query_row])
        bias = jnp.where(member & (key_rows >= 0), 0.0, big_negative)
        bias_ref[row * columns : (row + 1) * columns] = bias
    for move in moves:
        move.wait()


def staged(arrays, index, lists, blocks, space):
    _, rows, columns, _ = arrays[0].shape
    in_vmem = pl.BlockSpec(memory_space=pltpu.VMEM)
    bias = jax.ShapeDtypeStruct((rows * columns, blocks * rows * columns), jnp.float32)
    return pl.pallas_call(
        functools.partial(stage_kernel, blocks, space),
        out_shape=(bias, *[jax.ShapeDtypeStruct(a.shape, a.dtype) for a in arrays]),
        in_specs=[pl.BlockSpec(memory_space=pltpu.SMEM)] * 2
        + [pl.BlockSpec(memory_space=pl.ANY)] * len(arrays),
        out_specs=(in_vmem,) * (1 + len(arrays)),
        scratch_shapes=[pltpu.SemaphoreType.DMA((len(arrays),))],
        compiler_params=pltpu.CompilerParams(vmem_limit_bytes=53 * 1024 * 1024),
        cost_estimate=pl.CostEstimate(flops=1, bytes_accessed=1, transcendentals=0),
        name="stage",
    )(index, lists, *arrays)


def spatial_weigh_kernel(blocks, bias_ref, q_ref, *refs):
    k_refs, weights_ref, inverse_ref = refs[:blocks], *refs[-2:]
    bias = bias_ref[...]
    for frame in range(q_ref.shape[0]):

        def write_weights(head, value):
            weights_ref[frame, head] = value

        def write_inverse(lanes, value):
            inverse_ref[frame, :, lanes] = value

        weigh(
            q_ref.shape[-1],
            lambda lanes: read_tokens([q_ref], frame, lanes),
            lambda lanes: read_tokens(k_refs, frame, lanes),
            bias,
            write_weights,
            write_inverse,
        )


def read_weights(weights_ref, group, heads):
    _, _, rows, keys = weights_ref.shape
    return weights_ref[group, heads[0] : heads[-1] + 1].reshape(len(heads) * rows, keys)


def spatial_blend_kernel(blocks, weights_ref, inverse_ref, *refs):
    v_refs, (out_ref, held, sems) = refs[:blocks], refs[-3:]
    frames, rows, columns, channels = held.shape
    moves = []
    for frame in range(frames):
        sent = 0

        def write(lanes, value):
            nonlocal sent
            held[frame, :, :, lanes] = value.reshape(rows, columns, LANES)
            if lanes.stop in (channels // 2 // WINDOW * WINDOW, channels):
                part = (frame, slice(None), slice(None), slice(sent, lanes.stop))
                moves.append(
                    pltpu.make_async_copy(held.at[part], out_ref.at[part], sems.at[len(moves)])
                )
                moves[-1].start()
                sent = lanes.stop

        blend(
            channels,
            rows * columns,
            lambda heads: read_weights(weights_ref, frame, heads),
            lambda lanes: inverse_ref[frame, :, lanes],
            lambda lanes: read_tokens(v_refs, frame, lanes),
            write,
        )
    for move in moves:
        move.wait()


def temporal_weigh_kernel(blocks, q_ref, *refs):
    k_refs, weights_ref, inverse_ref = refs[:blocks], *refs[-2:]
    frames, rows, columns, channels = q_ref.shape
    shape = (frames * columns, sum(ref.shape[0] for ref in k_refs) * columns)
    own = lax.broadcasted_iota(jnp.int32, shape, 0) % columns
    other = lax.broadcasted_iota(jnp.int32, shape, 1) % columns
    bias = jnp.where(own == other, 0.0, big_negative)
    for row in range(rows):

        def write_weights(head, value):
            weights_ref[row, head] = value

        def write_inverse(lanes, value):
            inverse_ref[row, :, lanes] = value

        weigh(
            channels,
            lambda lanes: read_row([q_ref], row, lanes),
            lambda lanes: read_row(k_refs, row, lanes),
            bias,
            write_weights,
            write_inverse,
        )


def temporal_blend_kernel(blocks, weights_ref, inverse_ref, *refs):
    v_refs, (out_ref, held, sems) = refs[:blocks], refs[-3:]
    frames, rows, columns, channels = held.shape
    moves = []
    for row in range(rows):

        def write(lanes, value):
            held[:, row, :, lanes] = value.reshape(frames, columns, LANES)

        blend(
            channels,
            frames * columns,
            lambda heads: read_weights(weights_ref, row, heads),
            lambda lanes: inverse_ref[row, :, lanes],
            lambda lanes: read_row(v_refs, row, lanes),
            write,
        )
        moves.append(
            pltpu.make_async_copy(held.at[:, row], out_ref.at[:, row], sems.at[row])
        )
        moves[-1].start()
    for move in moves:
        move.wait()


def call(kernel, name, out_shape, scalars, arrays, flops, others=(), parts=0):
    in_vmem = pl.BlockSpec(memory_space=pltpu.VMEM)
    in_smem = pl.BlockSpec(memory_space=pltpu.SMEM)
    anywhere = pl.BlockSpec(memory_space=pl.ANY)
    return pl.pallas_call(
        kernel,
        out_shape=out_shape,
        in_specs=[in_smem] * len(scalars) + [in_vmem] * len(arrays) + [anywhere] * len(others),
        out_specs=jax.tree.map(lambda _: anywhere if parts else in_vmem, out_shape),
        scratch_shapes=[
            pltpu.VMEM(out_shape.shape, out_shape.dtype),
            pltpu.SemaphoreType.DMA((parts,)),
        ]
        if parts
        else [],
        compiler_params=pltpu.CompilerParams(vmem_limit_bytes=40 * 1024 * 1024),
        cost_estimate=pl.CostEstimate(
            flops=flops, bytes_accessed=1, transcendentals=0
        ),
        name=name,
    )(*scalars, *arrays, *others)


def join_kernel(count, *refs):
    out_ref = refs[-1]
    first = 0
    for ref in refs[:count]:
        out_ref[first : first + ref.shape[0]] = ref[...]
        first += ref.shape[0]


def joined(arrays, others):
    shape = (sum(a.shape[0] for a in arrays),) + arrays[0].shape[1:]
    return call(
        functools.partial(join_kernel, len(arrays)),
        "join",
        jax.ShapeDtypeStruct(shape, arrays[0].dtype),
        [],
        arrays,
        1,
        others,
    )


def weigh_shapes(groups, channels, queries, keys):
    heads = channels // HEAD_DIM
    return (
        jax.ShapeDtypeStruct((groups, heads, queries, keys), jnp.bfloat16),
        jax.ShapeDtypeStruct((groups, queries, channels), jnp.float32),
    )


def on_device(spatial_q, spatial_k, spatial_v, temporal_q, temporal_k, temporal_v, key_lists):
    frames, rows, columns, channels = spatial_q.shape
    space = lax.axis_size("space")
    reach = -(-(key_lists.shape[1] // 2) // rows)
    index = lax.axis_index("space").reshape(1)
    out_shape = jax.ShapeDtypeStruct(spatial_q.shape, jnp.bfloat16)
    tokens = frames * rows * columns
    first_step = lax.axis_size("tm") // 2

    exchanges = [(d, parity) for d in range(1, reach + 1) for parity in (1, 0)]
    blocks = 1 + len(exchanges)
    bias, own_q, own_k, own_tv = staged(
        [spatial_q, spatial_k, temporal_v], index, key_lists.T, blocks, space
    )

    def gathered(own, received, others):
        held, step = [own, received], first_step // 2
        while step:
            held = [joined(held, others)]
            held.append(swapped(held[0], "tm", step))
            step //= 2
        return held

    received_keys = swapped(temporal_k, "tm", first_step)
    received_values = swapped(own_tv, "tm", first_step)
    spatial_keys = [own_k] + [exchanged(spatial_k, *which) for which in exchanges]
    spatial_values = [spatial_v] + [
        exchanged(spatial_v, *which) for which in exchanges
    ]

    keys = blocks * rows * columns
    spatial_weights, spatial_inverse = call(
        functools.partial(spatial_weigh_kernel, blocks),
        "spatial_weigh",
        weigh_shapes(frames, channels, rows * columns, keys),
        [],
        [bias, own_q, *spatial_keys],
        1,
        [received_keys],
    )
    temporal_keys = gathered(temporal_k, received_keys, [spatial_weights])
    blocks = len(temporal_keys)
    keys = sum(k.shape[0] for k in temporal_keys) * columns
    temporal_weights, temporal_inverse = call(
        functools.partial(temporal_weigh_kernel, blocks),
        "temporal_weigh",
        weigh_shapes(rows, channels, frames * columns, keys),
        [],
        [temporal_q, *temporal_keys],
        1,
    )
    temporal_values = gathered(own_tv, received_values, [spatial_weights, *spatial_values[1:]])
    spatial_out = call(
        functools.partial(spatial_blend_kernel, len(spatial_values)),
        "spatial_blend",
        out_shape,
        [],
        [spatial_weights, spatial_inverse, *spatial_values],
        1,
        parts=2 * frames,
    )
    temporal_out = call(
        functools.partial(temporal_blend_kernel, blocks),
        "temporal_blend",
        out_shape,
        [],
        [temporal_weights, temporal_inverse, *temporal_values],
        1,
        parts=rows,
    )
    return (spatial_out, temporal_out)


def solution(mesh):
    placed = P(("video", "tm"), "space", None, None)
    return jax.shard_map(
        on_device,
        mesh=mesh,
        in_specs=(placed,) * 6 + (P(),),
        out_specs=(placed, placed),
        check_vma=False,
    )
```

```python
import functools
import math

import jax
import jax.numpy as jnp
from jax import lax
from jax.experimental import pallas as pl
from jax.experimental.pallas import tpu as pltpu
from jax.sharding import PartitionSpec as P

HEAD_DIM = 72
LANES = 128
WINDOW = 2 * LANES
SCALE = HEAD_DIM ** (-0.5) * math.log2(math.e)
big_negative = -1e30
AXES = ("space", "tm")


def partner_of(index, distance, parity):
    upward = (index // distance) % 2 == parity
    if isinstance(index, int):
        return index + distance if upward else index - distance
    return jnp.where(upward, index + distance, index - distance)


def exchanged(value, distance, parity):
    length, others = [lax.axis_size(axis) for axis in AXES]
    pairs = []
    for index in range(length):
        partner = partner_of(index, distance, parity)
        for other in range(others):
            if 0 <= partner < length:
                target = partner * others + other
            else:
                target = index * others + (other ^ 1 if (other ^ 1) < others else other)
            pairs.append((index * others + other, target))
    return lax.ppermute(value, AXES, pairs)


def swapped(value, axis, step):
    return lax.ppermute(value, axis, [(i, i ^ step) for i in range(lax.axis_size(axis))])


def windows_of(channels):
    windows = []
    for first in range(0, channels, WINDOW):
        last = min(first + WINDOW, channels)
        windows.append((slice(first, last), range(first // HEAD_DIM, (last - 1) // HEAD_DIM + 1)))
    return windows


def by_head(parts, heads, first, rows):
    lane = lax.broadcasted_iota(jnp.int32, (rows, LANES), 1) + first
    chosen = parts[0]
    for head, part in zip(heads[1:], parts[1:]):
        chosen = jnp.where(lane >= head * HEAD_DIM, part, chosen)
    return chosen


def tile_heads(first):
    return range(first // HEAD_DIM, (first + LANES - 1) // HEAD_DIM + 1)


def weigh(channels, read_queries, read_keys, bias, write_weights, write_inverse):
    scores, inverses = {}, {}
    rows = bias.shape[0]
    for lanes, heads in windows_of(channels):
        queries = read_queries(lanes)
        lane = lax.broadcasted_iota(jnp.int32, queries.shape, 1) + lanes.start
        stacked = []
        for head in heads:
            mask = (lane >= head * HEAD_DIM) & (lane < (head + 1) * HEAD_DIM)
            stacked.append(queries * mask.astype(jnp.bfloat16))
        both = lax.dot_general(
            jnp.concatenate(stacked, axis=0),
            read_keys(lanes),
            (((1,), (1,)), ((), ())),
            preferred_element_type=jnp.float32,
        )
        for place, head in enumerate(heads):
            part = both[place * rows : (place + 1) * rows]
            scores[head] = scores[head] + part if head in scores else part
            if (head + 1) * HEAD_DIM > lanes.stop:
                continue
            masked = scores.pop(head) * SCALE + bias
            highest = jnp.max(masked, axis=-1, keepdims=True)
            weights = jnp.exp2(masked - highest)
            inverses[head] = 1.0 / jnp.sum(weights, axis=-1, keepdims=True)
            write_weights(head, weights.astype(jnp.bfloat16))
    for first in range(0, channels, LANES):
        heads = tile_heads(first)
        parts = [jnp.broadcast_to(inverses[head], (rows, LANES)) for head in heads]
        write_inverse(slice(first, first + LANES), by_head(parts, heads, first, rows))


def blend(channels, rows, read_weights, read_inverse, read_values, write):
    blended = []
    for first in range(0, channels, LANES):
        heads = tile_heads(first)
        pair = first // LANES
        if first + WINDOW <= channels:
            values = read_values(slice(first, first + WINDOW))
            weights = read_weights(range(2 * pair, 2 * pair + 2))
            blended.append(jnp.dot(weights, values, preferred_element_type=jnp.float32))
        parts = []
        for head in heads:
            place, lane = head % 2 * rows, first - head // 2 * LANES
            parts.append(blended[head // 2][place : place + rows, lane : lane + LANES])
        tile = slice(first, first + LANES)
        chosen = by_head(parts, heads, first, rows) * read_inverse(tile)
        write(tile, chosen.astype(jnp.bfloat16))


def read_tokens(refs, frame, lanes):
    return jnp.concatenate(
        [ref[frame, :, :, lanes].reshape(-1, lanes.stop - lanes.start) for ref in refs], axis=0
    )


def read_row(refs, row, lanes):
    return jnp.concatenate(
        [ref[:, row, :, lanes].reshape(-1, lanes.stop - lanes.start) for ref in refs], axis=0
    )


def stage_kernel(blocks, space, index_ref, lists_ref, *refs):
    count = (len(refs) - 2) // 2
    sources, bias_ref, copies, sems = refs[:count], refs[count], refs[count + 1 : -1], refs[-1]
    moves = [
        pltpu.make_async_copy(source, copy, sems.at[i])
        for i, (source, copy) in enumerate(zip(sources, copies))
    ]
    for move in moves:
        move.start()
    _, rows, columns, _ = sources[0].shape
    index = index_ref[0]
    key_rows = []
    for distance in range(blocks // 2 + 1):
        for parity in (0, 1) if distance else (0,):
            owner = partner_of(index, distance, parity) if distance else index
            first = jnp.where((owner >= 0) & (owner < space), owner * rows, -(2**20))
            row = lax.broadcasted_iota(jnp.int32, (columns, rows * columns), 1) // columns
            key_rows.append(row + first)
    key_rows = jnp.concatenate(key_rows, axis=1)
    for row in range(rows):
        query_row = index * rows + row
        member = key_rows == query_row
        for entry in range(lists_ref.shape[0]):
            member = member | (key_rows == lists_ref[entry, query_row])
        bias = jnp.where(member & (key_rows >= 0), 0.0, big_negative)
        bias_ref[row * columns : (row + 1) * columns] = bias
    for move in moves:
        move.wait()


def staged(arrays, index, lists, blocks, space):
    _, rows, columns, _ = arrays[0].shape
    in_vmem = pl.BlockSpec(memory_space=pltpu.VMEM)
    bias = jax.ShapeDtypeStruct((rows * columns, blocks * rows * columns), jnp.float32)
    return pl.pallas_call(
        functools.partial(stage_kernel, blocks, space),
        out_shape=(bias, *[jax.ShapeDtypeStruct(a.shape, a.dtype) for a in arrays]),
        in_specs=[pl.BlockSpec(memory_space=pltpu.SMEM)] * 2
        + [pl.BlockSpec(memory_space=pl.ANY)] * len(arrays),
        out_specs=(in_vmem,) * (1 + len(arrays)),
        scratch_shapes=[pltpu.SemaphoreType.DMA((len(arrays),))],
        compiler_params=pltpu.CompilerParams(vmem_limit_bytes=53 * 1024 * 1024),
        cost_estimate=pl.CostEstimate(flops=1, bytes_accessed=1, transcendentals=0),
        name="stage",
    )(index, lists, *arrays)


def spatial_weigh_kernel(blocks, bias_ref, q_ref, *refs):
    k_refs, weights_ref, inverse_ref = refs[:blocks], *refs[-2:]
    bias = bias_ref[...]
    for frame in range(q_ref.shape[0]):

        def write_weights(head, value):
            weights_ref[frame, head] = value

        def write_inverse(lanes, value):
            inverse_ref[frame, :, lanes] = value

        weigh(
            q_ref.shape[-1],
            lambda lanes: read_tokens([q_ref], frame, lanes),
            lambda lanes: read_tokens(k_refs, frame, lanes),
            bias,
            write_weights,
            write_inverse,
        )


def read_weights(weights_ref, group, heads):
    _, _, rows, keys = weights_ref.shape
    return weights_ref[group, heads[0] : heads[-1] + 1].reshape(len(heads) * rows, keys)


def spatial_blend_kernel(blocks, weights_ref, inverse_ref, *refs):
    v_refs, out_ref = refs[:blocks], refs[-1]
    frames, rows, columns, channels = out_ref.shape
    for frame in range(frames):

        def write(lanes, value):
            out_ref[frame, :, :, lanes] = value.reshape(rows, columns, LANES)

        blend(
            channels,
            rows * columns,
            lambda heads: read_weights(weights_ref, frame, heads),
            lambda lanes: inverse_ref[frame, :, lanes],
            lambda lanes: read_tokens(v_refs, frame, lanes),
            write,
        )


def temporal_weigh_kernel(blocks, q_ref, *refs):
    k_refs, weights_ref, inverse_ref = refs[:blocks], *refs[-2:]
    frames, rows, columns, channels = q_ref.shape
    shape = (frames * columns, sum(ref.shape[0] for ref in k_refs) * columns)
    own = lax.broadcasted_iota(jnp.int32, shape, 0) % columns
    other = lax.broadcasted_iota(jnp.int32, shape, 1) % columns
    bias = jnp.where(own == other, 0.0, big_negative)
    for row in range(rows):

        def write_weights(head, value):
            weights_ref[row, head] = value

        def write_inverse(lanes, value):
            inverse_ref[row, :, lanes] = value

        weigh(
            channels,
            lambda lanes: read_row([q_ref], row, lanes),
            lambda lanes: read_row(k_refs, row, lanes),
            bias,
            write_weights,
            write_inverse,
        )


def last_kernel(blocks, spatial_ref, weights_ref, inverse_ref, *refs):
    v_refs, (spatial_out_ref, out_ref, held, sems) = refs[:blocks], refs[-4:]
    frames, rows, columns, channels = held.shape
    moves = [pltpu.make_async_copy(spatial_ref, spatial_out_ref, sems.at[rows])]
    moves[-1].start()
    for row in range(rows):

        def write(lanes, value):
            held[:, row, :, lanes] = value.reshape(frames, columns, LANES)

        blend(
            channels,
            frames * columns,
            lambda heads: read_weights(weights_ref, row, heads),
            lambda lanes: inverse_ref[row, :, lanes],
            lambda lanes: read_row(v_refs, row, lanes),
            write,
        )
        moves.append(
            pltpu.make_async_copy(held.at[:, row], out_ref.at[:, row], sems.at[row])
        )
        moves[-1].start()
    for move in moves:
        move.wait()


def call(kernel, name, out_shape, scalars, arrays, flops, others=(), held=(), sems=0):
    in_vmem = pl.BlockSpec(memory_space=pltpu.VMEM)
    in_smem = pl.BlockSpec(memory_space=pltpu.SMEM)
    anywhere = pl.BlockSpec(memory_space=pl.ANY)
    return pl.pallas_call(
        kernel,
        out_shape=out_shape,
        in_specs=[in_smem] * len(scalars) + [in_vmem] * len(arrays) + [anywhere] * len(others),
        out_specs=jax.tree.map(lambda _: anywhere if sems else in_vmem, out_shape),
        scratch_shapes=[*held, pltpu.SemaphoreType.DMA((sems,))] if sems else [],
        compiler_params=pltpu.CompilerParams(vmem_limit_bytes=40 * 1024 * 1024),
        cost_estimate=pl.CostEstimate(
            flops=flops, bytes_accessed=1, transcendentals=0
        ),
        name=name,
    )(*scalars, *arrays, *others)


def join_kernel(count, *refs):
    out_ref = refs[-1]
    first = 0
    for ref in refs[:count]:
        out_ref[first : first + ref.shape[0]] = ref[...]
        first += ref.shape[0]


def joined(arrays, others):
    shape = (sum(a.shape[0] for a in arrays),) + arrays[0].shape[1:]
    return call(
        functools.partial(join_kernel, len(arrays)),
        "join",
        jax.ShapeDtypeStruct(shape, arrays[0].dtype),
        [],
        arrays,
        1,
        others,
    )


def weigh_shapes(groups, channels, queries, keys):
    heads = channels // HEAD_DIM
    return (
        jax.ShapeDtypeStruct((groups, heads, queries, keys), jnp.bfloat16),
        jax.ShapeDtypeStruct((groups, queries, channels), jnp.float32),
    )


def on_device(spatial_q, spatial_k, spatial_v, temporal_q, temporal_k, temporal_v, key_lists):
    frames, rows, columns, channels = spatial_q.shape
    space = lax.axis_size("space")
    reach = -(-(key_lists.shape[1] // 2) // rows)
    index = lax.axis_index("space").reshape(1)
    out_shape = jax.ShapeDtypeStruct(spatial_q.shape, jnp.bfloat16)
    tokens = frames * rows * columns
    first_step = lax.axis_size("tm") // 2

    exchanges = [(d, parity) for d in range(1, reach + 1) for parity in (0, 1)]
    blocks = 1 + len(exchanges)
    bias, own_q, own_k, own_tv = staged(
        [spatial_q, spatial_k, temporal_v], index, key_lists.T, blocks, space
    )

    def gathered(own, received, others):
        held, step = [own, received], first_step // 2
        while step:
            held = [joined(held, others)]
            held.append(swapped(held[0], "tm", step))
            step //= 2
        return held

    received_keys = swapped(temporal_k, "tm", first_step)
    received_values = swapped(own_tv, "tm", first_step)
    spatial_keys = [own_k] + [exchanged(spatial_k, *which) for which in exchanges]
    spatial_values = [spatial_v] + [
        exchanged(spatial_v, *which) for which in exchanges
    ]

    keys = blocks * rows * columns
    spatial_weights, spatial_inverse = call(
        functools.partial(spatial_weigh_kernel, blocks),
        "spatial_weigh",
        weigh_shapes(frames, channels, rows * columns, keys),
        [],
        [bias, own_q, *spatial_keys],
        1,
        [received_keys],
    )
    temporal_keys = gathered(temporal_k, received_keys, [spatial_weights])
    blocks = len(temporal_keys)
    keys = sum(k.shape[0] for k in temporal_keys) * columns
    temporal_weights, temporal_inverse = call(
        functools.partial(temporal_weigh_kernel, blocks),
        "temporal_weigh",
        weigh_shapes(rows, channels, frames * columns, keys),
        [],
        [temporal_q, *temporal_keys],
        1,
    )
    temporal_values = gathered(own_tv, received_values, [spatial_weights, *spatial_values[1:]])
    spatial_result = call(
        functools.partial(spatial_blend_kernel, len(spatial_values)),
        "spatial_blend",
        out_shape,
        [],
        [spatial_weights, spatial_inverse, *spatial_values],
        1,
    )
    return call(
        functools.partial(last_kernel, len(temporal_values)),
        "last",
        (out_shape, out_shape),
        [],
        [spatial_result, temporal_weights, temporal_inverse, *temporal_values],
        1,
        held=[pltpu.VMEM(out_shape.shape, out_shape.dtype)],
        sems=rows + 1,
    )


def solution(mesh):
    placed = P(("video", "tm"), "space", None, None)
    return jax.shard_map(
        on_device,
        mesh=mesh,
        in_specs=(placed,) * 6 + (P(),),
        out_specs=(placed, placed),
        check_vma=False,
    )
```

```python
import functools
import math

import jax
import jax.numpy as jnp
from jax import lax
from jax.experimental import pallas as pl
from jax.experimental.pallas import tpu as pltpu
from jax.sharding import PartitionSpec as P

HEAD_DIM = 72
LANES = 128
WINDOW = 2 * LANES
SCALE = HEAD_DIM ** (-0.5) * math.log2(math.e)
big_negative = -1e30
AXES = ("space", "tm")


def partner_of(index, distance, parity):
    upward = (index // distance) % 2 == parity
    if isinstance(index, int):
        return index + distance if upward else index - distance
    return jnp.where(upward, index + distance, index - distance)


def exchanged(value, distance, parity):
    length, others = [lax.axis_size(axis) for axis in AXES]
    pairs = []
    for index in range(length):
        partner = partner_of(index, distance, parity)
        for other in range(others):
            if 0 <= partner < length:
                target = partner * others + other
            else:
                target = index * others + (other ^ 1 if (other ^ 1) < others else other)
            pairs.append((index * others + other, target))
    return lax.ppermute(value, AXES, pairs)


def swapped(value, axis, step):
    return lax.ppermute(value, axis, [(i, i ^ step) for i in range(lax.axis_size(axis))])


def windows_of(channels):
    windows = []
    for first in range(0, channels, WINDOW):
        last = min(first + WINDOW, channels)
        windows.append((slice(first, last), range(first // HEAD_DIM, (last - 1) // HEAD_DIM + 1)))
    return windows


def by_head(parts, heads, first, rows):
    lane = lax.broadcasted_iota(jnp.int32, (rows, LANES), 1) + first
    chosen = parts[0]
    for head, part in zip(heads[1:], parts[1:]):
        chosen = jnp.where(lane >= head * HEAD_DIM, part, chosen)
    return chosen


def tile_heads(first):
    return range(first // HEAD_DIM, (first + LANES - 1) // HEAD_DIM + 1)


def weigh(channels, read_queries, read_keys, bias, write_weights, write_inverse):
    scores, inverses = {}, {}
    rows = bias.shape[0]
    for lanes, heads in windows_of(channels):
        queries = read_queries(lanes)
        lane = lax.broadcasted_iota(jnp.int32, queries.shape, 1) + lanes.start
        stacked = []
        for head in heads:
            mask = (lane >= head * HEAD_DIM) & (lane < (head + 1) * HEAD_DIM)
            stacked.append(queries * mask.astype(jnp.bfloat16))
        both = lax.dot_general(
            jnp.concatenate(stacked, axis=0),
            read_keys(lanes),
            (((1,), (1,)), ((), ())),
            preferred_element_type=jnp.float32,
        )
        for place, head in enumerate(heads):
            part = both[place * rows : (place + 1) * rows]
            scores[head] = scores[head] + part if head in scores else part
            if (head + 1) * HEAD_DIM > lanes.stop:
                continue
            masked = scores.pop(head) * SCALE + bias
            highest = jnp.max(masked, axis=-1, keepdims=True)
            weights = jnp.exp2(masked - highest)
            inverses[head] = 1.0 / jnp.sum(weights, axis=-1, keepdims=True)
            write_weights(head, weights.astype(jnp.bfloat16))
    for first in range(0, channels, LANES):
        heads = tile_heads(first)
        parts = [jnp.broadcast_to(inverses[head], (rows, LANES)) for head in heads]
        write_inverse(slice(first, first + LANES), by_head(parts, heads, first, rows))


def blend(channels, rows, read_weights, read_inverse, read_values, write):
    blended = []
    for first in range(0, channels, LANES):
        heads = tile_heads(first)
        pair = first // LANES
        if first + WINDOW <= channels:
            values = read_values(slice(first, first + WINDOW))
            weights = read_weights(range(2 * pair, 2 * pair + 2))
            blended.append(jnp.dot(weights, values, preferred_element_type=jnp.float32))
        parts = []
        for head in heads:
            place, lane = head % 2 * rows, first - head // 2 * LANES
            parts.append(blended[head // 2][place : place + rows, lane : lane + LANES])
        tile = slice(first, first + LANES)
        chosen = by_head(parts, heads, first, rows) * read_inverse(tile)
        write(tile, chosen.astype(jnp.bfloat16))


def read_tokens(refs, frame, lanes):
    return jnp.concatenate(
        [ref[frame, :, :, lanes].reshape(-1, lanes.stop - lanes.start) for ref in refs], axis=0
    )


def read_row(refs, row, lanes):
    return jnp.concatenate(
        [ref[:, row, :, lanes].reshape(-1, lanes.stop - lanes.start) for ref in refs], axis=0
    )


def stage_kernel(blocks, space, index_ref, lists_ref, *refs):
    count = (len(refs) - 2) // 2
    sources, bias_ref, copies, sems = refs[:count], refs[count], refs[count + 1 : -1], refs[-1]
    moves = [
        pltpu.make_async_copy(source, copy, sems.at[i])
        for i, (source, copy) in enumerate(zip(sources, copies))
    ]
    for move in moves:
        move.start()
    _, rows, columns, _ = sources[0].shape
    index = index_ref[0]
    key_rows = []
    for distance in range(blocks // 2 + 1):
        for parity in (0, 1) if distance else (0,):
            owner = partner_of(index, distance, parity) if distance else index
            first = jnp.where((owner >= 0) & (owner < space), owner * rows, -(2**20))
            row = lax.broadcasted_iota(jnp.int32, (columns, rows * columns), 1) // columns
            key_rows.append(row + first)
    key_rows = jnp.concatenate(key_rows, axis=1)
    for row in range(rows):
        query_row = index * rows + row
        member = key_rows == query_row
        for entry in range(lists_ref.shape[0]):
            member = member | (key_rows == lists_ref[entry, query_row])
        bias = jnp.where(member & (key_rows >= 0), 0.0, big_negative)
        bias_ref[row * columns : (row + 1) * columns] = bias
    for move in moves:
        move.wait()


def staged(arrays, index, lists, blocks, space):
    _, rows, columns, _ = arrays[0].shape
    in_vmem = pl.BlockSpec(memory_space=pltpu.VMEM)
    bias = jax.ShapeDtypeStruct((rows * columns, blocks * rows * columns), jnp.float32)
    return pl.pallas_call(
        functools.partial(stage_kernel, blocks, space),
        out_shape=(bias, *[jax.ShapeDtypeStruct(a.shape, a.dtype) for a in arrays]),
        in_specs=[pl.BlockSpec(memory_space=pltpu.SMEM)] * 2
        + [pl.BlockSpec(memory_space=pl.ANY)] * len(arrays),
        out_specs=(in_vmem,) * (1 + len(arrays)),
        scratch_shapes=[pltpu.SemaphoreType.DMA((len(arrays),))],
        compiler_params=pltpu.CompilerParams(vmem_limit_bytes=53*1024*1024),
        cost_estimate=pl.CostEstimate(flops=1, bytes_accessed=1, transcendentals=0),
        name="stage",
    )(index, lists, *arrays)


def spatial_weigh_kernel(blocks, bias_ref, q_ref, *refs):
    k_refs, weights_ref, inverse_ref = refs[:blocks], *refs[-2:]
    bias = bias_ref[...]
    for frame in range(q_ref.shape[0]):

        def write_weights(head, value):
            weights_ref[frame, head] = value

        def write_inverse(lanes, value):
            inverse_ref[frame, :, lanes] = value

        weigh(
            q_ref.shape[-1],
            lambda lanes: read_tokens([q_ref], frame, lanes),
            lambda lanes: read_tokens(k_refs, frame, lanes),
            bias,
            write_weights,
            write_inverse,
        )


def read_weights(weights_ref, group, heads):
    _, _, rows, keys = weights_ref.shape
    return weights_ref[group, heads[0] : heads[-1] + 1].reshape(len(heads) * rows, keys)


def spatial_blend_kernel(blocks, weights_ref, inverse_ref, *refs):
    v_refs, out_ref = refs[:blocks], refs[-1]
    frames, rows, columns, channels = out_ref.shape
    for frame in range(frames):

        def write(lanes, value):
            out_ref[frame, :, :, lanes] = value.reshape(rows, columns, LANES)

        blend(
            channels,
            rows * columns,
            lambda heads: read_weights(weights_ref, frame, heads),
            lambda lanes: inverse_ref[frame, :, lanes],
            lambda lanes: read_tokens(v_refs, frame, lanes),
            write,
        )


def temporal_weigh_kernel(blocks, q_ref, *refs):
    k_refs, weights_ref, inverse_ref = refs[:blocks], *refs[-2:]
    frames, rows, columns, channels = q_ref.shape
    shape = (frames * columns, sum(ref.shape[0] for ref in k_refs) * columns)
    own = lax.broadcasted_iota(jnp.int32, shape, 0) % columns
    other = lax.broadcasted_iota(jnp.int32, shape, 1) % columns
    bias = jnp.where(own == other, 0.0, big_negative)
    for row in range(rows):

        def write_weights(head, value):
            weights_ref[row, head] = value

        def write_inverse(lanes, value):
            inverse_ref[row, :, lanes] = value

        weigh(
            channels,
            lambda lanes: read_row([q_ref], row, lanes),
            lambda lanes: read_row(k_refs, row, lanes),
            bias,
            write_weights,
            write_inverse,
        )


def last_kernel(blocks, spatial_ref, weights_ref, inverse_ref, *refs):
    v_refs, (spatial_out_ref, out_ref, held, sems) = refs[:blocks], refs[-4:]
    frames, rows, columns, channels = held.shape
    moves = [pltpu.make_async_copy(spatial_ref, spatial_out_ref, sems.at[rows])]
    moves[-1].start()
    for row in range(rows):

        def write(lanes, value):
            held[:, row, :, lanes] = value.reshape(frames, columns, LANES)

        blend(
            channels,
            frames * columns,
            lambda heads: read_weights(weights_ref, row, heads),
            lambda lanes: inverse_ref[row, :, lanes],
            lambda lanes: read_row(v_refs, row, lanes),
            write,
        )
        moves.append(
            pltpu.make_async_copy(held.at[:, row], out_ref.at[:, row], sems.at[row])
        )
        moves[-1].start()
    for move in moves:
        move.wait()


def call(kernel, name, out_shape, scalars, arrays, flops, others=(), held=(), sems=0):
    in_vmem = pl.BlockSpec(memory_space=pltpu.VMEM)
    in_smem = pl.BlockSpec(memory_space=pltpu.SMEM)
    anywhere = pl.BlockSpec(memory_space=pl.ANY)
    return pl.pallas_call(
        kernel,
        out_shape=out_shape,
        in_specs=[in_smem] * len(scalars) + [in_vmem] * len(arrays) + [anywhere] * len(others),
        out_specs=jax.tree.map(lambda _: anywhere if sems else in_vmem, out_shape),
        scratch_shapes=[*held, pltpu.SemaphoreType.DMA((sems,))] if sems else [],
        compiler_params=pltpu.CompilerParams(vmem_limit_bytes=40 * 1024 * 1024),
        cost_estimate=pl.CostEstimate(
            flops=flops, bytes_accessed=1, transcendentals=0
        ),
        name=name,
    )(*scalars, *arrays, *others)


def join_kernel(count, *refs):
    out_ref = refs[-1]
    first = 0
    for ref in refs[:count]:
        out_ref[first : first + ref.shape[0]] = ref[...]
        first += ref.shape[0]


def joined(arrays, others):
    shape = (sum(a.shape[0] for a in arrays),) + arrays[0].shape[1:]
    return call(
        functools.partial(join_kernel, len(arrays)),
        "join",
        jax.ShapeDtypeStruct(shape, arrays[0].dtype),
        [],
        arrays,
        1,
        others,
    )


def weigh_shapes(groups, channels, queries, keys):
    heads = channels // HEAD_DIM
    return (
        jax.ShapeDtypeStruct((groups, heads, queries, keys), jnp.bfloat16),
        jax.ShapeDtypeStruct((groups, queries, channels), jnp.float32),
    )


def on_device(spatial_q, spatial_k, spatial_v, temporal_q, temporal_k, temporal_v, key_lists):
    frames, rows, columns, channels = spatial_q.shape
    space = lax.axis_size("space")
    reach = -(-(key_lists.shape[1] // 2) // rows)
    index = lax.axis_index("space").reshape(1)
    out_shape = jax.ShapeDtypeStruct(spatial_q.shape, jnp.bfloat16)
    tokens = frames * rows * columns
    first_step = lax.axis_size("tm") // 2

    exchanges = [(d, parity) for d in range(1, reach + 1) for parity in (0, 1)]
    blocks = 1 + len(exchanges)
    bias, own_q, own_k, own_v = staged(
        [spatial_q, spatial_k, spatial_v], index, key_lists.T, blocks, space
    )

    def gathered(own, received, others):
        held, step = [own, received], first_step // 2
        while step:
            held = [joined(held, others)]
            held.append(swapped(held[0], "tm", step))
            step //= 2
        return held

    received_keys = swapped(temporal_k, "tm", first_step)
    received_values = swapped(temporal_v, "tm", first_step)
    spatial_keys = [own_k] + [exchanged(spatial_k, *which) for which in exchanges]
    spatial_values = [own_v] + [
        exchanged(own_v if which[1] == 0 else spatial_v, *which) for which in exchanges
    ]

    keys = blocks * rows * columns
    spatial_weights, spatial_inverse = call(
        functools.partial(spatial_weigh_kernel, blocks),
        "spatial_weigh",
        weigh_shapes(frames, channels, rows * columns, keys),
        [],
        [bias, own_q, *spatial_keys],
        1,
        [received_keys],
    )
    temporal_keys = gathered(temporal_k, received_keys, [spatial_weights])
    blocks = len(temporal_keys)
    keys = sum(k.shape[0] for k in temporal_keys) * columns
    temporal_weights, temporal_inverse = call(
        functools.partial(temporal_weigh_kernel, blocks),
        "temporal_weigh",
        weigh_shapes(rows, channels, frames * columns, keys),
        [],
        [temporal_q, *temporal_keys],
        1,
    )
    temporal_values = gathered(temporal_v, received_values, [spatial_weights])
    spatial_result = call(
        functools.partial(spatial_blend_kernel, len(spatial_values)),
        "spatial_blend",
        out_shape,
        [],
        [spatial_weights, spatial_inverse, *spatial_values],
        10**11,
    )
    return call(
        functools.partial(last_kernel, len(temporal_values)),
        "last",
        (out_shape, out_shape),
        [],
        [spatial_result, temporal_weights, temporal_inverse, *temporal_values],
        1,
        held=[pltpu.VMEM(out_shape.shape, out_shape.dtype)],
        sems=rows + 1,
    )


def solution(mesh):
    placed = P(("video", "tm"), "space", None, None)
    return jax.shard_map(
        on_device,
        mesh=mesh,
        in_specs=(placed,) * 6 + (P(),),
        out_specs=(placed, placed),
        check_vma=False,
    )
```
